512 devices in a mesh: head: 8 (over x, core), ctx: 64 (over z, y).
Axes of the slice: x: 4, y: 4, z: 16, core: 2. Of those that a mesh axis runs over, the one named last changes fastest.
Arguments:
- queries: bfloat16 [32768, 8192], P(('ctx', 'head')), may hold values from -6 to 6
- outputs: bfloat16 [32768, 8192], P(('ctx', 'head')), may hold values from -6 to 6
- output_gradient: bfloat16 [32768, 8192], P(('ctx', 'head')), may hold values from -6 to 6
- keys: bfloat16 [32768, 1024], P(('ctx', 'head')), may hold values from -6 to 6
- values: bfloat16 [32768, 1024], P(('ctx', 'head')), may hold values from -6 to 6
- log_row_norm: float32 [32768, 64], P(('ctx', 'head')), may hold values from 4 to 7
- kv_index: int32 [256, 10], replicated, may hold values from 0 to 255, as said below
- counts: int32 [256], replicated, may hold values from 1 to 10
Outputs:
- grad_queries: bfloat16 [32768, 8192], P(('ctx', 'head'))
- key_gradient: bfloat16 [32768, 1024], P(('ctx', 'head'))
- value_gradient: bfloat16 [32768, 1024], P(('ctx', 'head'))
The draws below stay inside these ranges and needn't reach their ends.
Inputs may be any that keep to these rules, and one draw needn't show every extreme that they name: `kv_index`: row i lists distinct tiles of index at most i in rising order in its first counts[i] entries: always i, i - 1 when i >= 1, and tile 3 when i >= 3, besides others; the remaining entries are 0. Tile t lies on ctx index t // 4. Taken together, the rows of the tiles of one ctx index name at most one tile of each other ctx index.
All inputs are finite; a program needn't handle non-finite values.
Results may differ from the reference program's by a relative error of at most 0.0049.
Values may be sent and summed in bfloat16 or wider, within the bound.
A program may use at most 128 MiB of HBM per device.

```python
import jax
import jax.numpy as jnp
from jax import lax

QUERY_HEADS = 64
KEY_VALUE_HEADS = 8
HEAD_SIZE = 128
TILE_TOKENS = 128
TILES_DEV = 4
SEQUENCE_TILES = 256
SEQUENCE_TOKENS = 32768
RMAX = 7
MAXB = 10


def layout(key):
    nodes = SEQUENCE_TILES // TILES_DEV
    base = jax.random.fold_in(key, 7)
    keys_list = jax.random.split(base, 3)
    device = jnp.arange(nodes, dtype=jnp.int32)
    eligible = (device[None, :] >= 1) & (device[None, :] <= device[:, None] - 2)
    priority = jax.random.randint(keys_list[0], (nodes, nodes), 0, 4096) * nodes + device[None, :]
    earlier = eligible[:, None, :] & (priority[:, None, :] < priority[:, :, None])
    ahead = jnp.sum(earlier.astype(jnp.int32), axis=2)
    full_quota = TILES_DEV * RMAX
    quota = jax.random.randint(keys_list[2], (nodes,), full_quota // 2, full_quota + 1)
    quota = jnp.where(device == nodes - 1, full_quota, quota)
    chosen = eligible & (ahead < quota[:, None])
    owner_tile = ahead % TILES_DEV
    picked = jax.random.randint(keys_list[1], (nodes, nodes), 0, TILES_DEV)
    within = jnp.arange(TILES_DEV, dtype=jnp.int32)
    random_use = chosen[:, None, :, None] & (owner_tile[:, None, :, None] == within[None, :, None, None]) & (picked[:, None, :, None] == within[None, None, None, :])
    random_use = random_use.reshape(SEQUENCE_TILES, SEQUENCE_TILES)
    rows = jnp.arange(SEQUENCE_TILES, dtype=jnp.int32)[:, None]
    columns = jnp.arange(SEQUENCE_TILES, dtype=jnp.int32)[None, :]
    uses = random_use | (columns == rows) | (columns == rows - 1) | (columns == TILES_DEV - 1) & (rows >= TILES_DEV - 1)
    running_totals = jnp.sum(uses.astype(jnp.int32), axis=1)
    scores = jnp.where(uses, columns, SEQUENCE_TILES)
    ordered = jnp.sort(scores, axis=1)[:, :MAXB]
    listing = jnp.where(ordered < SEQUENCE_TILES, ordered, 0)
    return (listing.astype(jnp.int32), running_totals.astype(jnp.int32))


def draw_kv_index(key, part):
    listing, running_totals = layout(key)
    return listing


def draw_counts(key, part):
    listing, running_totals = layout(key)
    return running_totals


def shard_levels(stream_key, extent, cuts, least, high):
    loudness, own = 1.0, jax.random.fold_in(stream_key, 6)
    for dim, parts in cuts:
        steps = jnp.exp(jax.random.uniform(jax.random.fold_in(own, dim), (parts,), jnp.float32, least / len(cuts), high / len(cuts)))
        loudness = loudness * jnp.repeat(steps, extent[dim] // parts).reshape([-1 if axis == dim else 1 for axis in range(len(extent))])
    return loudness


def noise(stream_key, dims, spread, limit, cuts=(), held_as=jnp.bfloat16):
    drawn = jax.random.normal(stream_key, dims, jnp.float32) * spread
    if len(cuts) > 0:
        drawn = shard_levels(stream_key, dims, cuts, -0.22, 0.18) * drawn
    return jnp.clip(drawn, min=-limit, max=limit).astype(held_as)


def setup_inputs(seed: int = 0) -> dict:
    arg_keys = jax.random.split(jax.random.key(seed), 9)
    queries = noise(arg_keys[0], (SEQUENCE_TOKENS, QUERY_HEADS * HEAD_SIZE), 1.0, 6.0, ((0, 512),))
    outputs = noise(arg_keys[1], (SEQUENCE_TOKENS, QUERY_HEADS * HEAD_SIZE), 1.0, 6.0, ((0, 512),))
    output_gradient = noise(arg_keys[2], (SEQUENCE_TOKENS, QUERY_HEADS * HEAD_SIZE), 1.0, 6.0, ((0, 512),))
    keys = noise(arg_keys[3], (SEQUENCE_TOKENS, KEY_VALUE_HEADS * HEAD_SIZE), 1.0, 6.0, ((0, 512),))
    values = noise(arg_keys[4], (SEQUENCE_TOKENS, KEY_VALUE_HEADS * HEAD_SIZE), 1.0, 6.0, ((0, 512),))
    log_row_norm = jnp.clip(4.0 + 3.0 * jax.random.uniform(arg_keys[5], (SEQUENCE_TOKENS, QUERY_HEADS), jnp.float32) ** shard_levels(arg_keys[5], (SEQUENCE_TOKENS, QUERY_HEADS), ((0, 512),), -0.2, 0.2), 4.0, 7.0)
    kv_index = draw_kv_index(jax.random.fold_in(arg_keys[8], 71), 0)
    counts = draw_counts(jax.random.fold_in(arg_keys[8], 71), 0)
    return {"queries": queries, "outputs": outputs, "output_gradient": output_gradient, "keys": keys, "values": values, "log_row_norm": log_row_norm, "kv_index": kv_index, "counts": counts}


def pairwise_terms(query_row_block, gradient_rows, row_norm_block, delta_row_block, pair_tile, on_diagonal, kv_heads):
    scale_factor = HEAD_SIZE ** -0.5
    key_value = pair_tile.reshape(TILE_TOKENS, kv_heads, 2 * HEAD_SIZE).astype(jnp.float32)
    key_part = key_value[:, :, :HEAD_SIZE]
    value_part = key_value[:, :, HEAD_SIZE:]
    query_float = query_row_block.astype(jnp.float32)
    grad_float = gradient_rows.astype(jnp.float32)
    scores = jnp.einsum('qagd,kad->agqk', query_float, key_part) * scale_factor
    positions = jnp.arange(TILE_TOKENS, dtype=jnp.int32)
    allowed = (positions[None, :] <= positions[:, None]) | jnp.logical_not(on_diagonal)
    norm_shift = jnp.transpose(row_norm_block, (1, 2, 0))[:, :, :, None]
    weights = jnp.where(allowed, jnp.exp(scores - norm_shift), jnp.float32(0.0))
    rounded = lax.optimization_barrier(weights.astype(jnp.bfloat16)).astype(jnp.float32)
    value_grad = jnp.einsum('agqk,qagd->kad', rounded, grad_float)
    prob_grad = jnp.einsum('qagd,kad->agqk', grad_float, value_part)
    delta_shift = jnp.transpose(delta_row_block, (1, 2, 0))[:, :, :, None]
    score_grad = lax.optimization_barrier((weights * (prob_grad - delta_shift)).astype(jnp.bfloat16)).astype(jnp.float32)
    query_gradient = scale_factor * jnp.einsum('agqk,kad->qagd', score_grad, key_part)
    key_grad = scale_factor * jnp.einsum('agqk,qagd->kad', score_grad, query_float)
    pairwise_gradient = jnp.concatenate([key_grad, value_grad], axis=2).reshape(TILE_TOKENS, kv_heads * 2 * HEAD_SIZE)
    return query_gradient, pairwise_gradient


def reference(queries, outputs, output_gradient, keys, values, log_row_norm, kv_index, counts):
    query_group = QUERY_HEADS // KEY_VALUE_HEADS
    query_tile_block = queries.reshape(SEQUENCE_TILES, TILE_TOKENS, KEY_VALUE_HEADS, query_group, HEAD_SIZE)
    gradient_tiles = output_gradient.reshape(SEQUENCE_TILES, TILE_TOKENS, KEY_VALUE_HEADS, query_group, HEAD_SIZE)
    delta_value = jnp.sum(output_gradient.astype(jnp.float32).reshape(SEQUENCE_TOKENS, QUERY_HEADS, HEAD_SIZE) * outputs.astype(jnp.float32).reshape(SEQUENCE_TOKENS, QUERY_HEADS, HEAD_SIZE), axis=2)
    delta_tile_block = delta_value.reshape(SEQUENCE_TILES, TILE_TOKENS, KEY_VALUE_HEADS, query_group)
    tile_norm_block = log_row_norm.reshape(SEQUENCE_TILES, TILE_TOKENS, KEY_VALUE_HEADS, query_group)
    pairwise_tiles = jnp.concatenate([keys.reshape(SEQUENCE_TILES, TILE_TOKENS, KEY_VALUE_HEADS, HEAD_SIZE), values.reshape(SEQUENCE_TILES, TILE_TOKENS, KEY_VALUE_HEADS, HEAD_SIZE)], axis=3).reshape(SEQUENCE_TILES, TILE_TOKENS, KEY_VALUE_HEADS * 2 * HEAD_SIZE)

    def tile_step(running_totals, query_tile_index):
        query_row_block = query_tile_block[query_tile_index]
        gradient_rows = gradient_tiles[query_tile_index]
        row_norm_block = tile_norm_block[query_tile_index]
        delta_row_block = delta_tile_block[query_tile_index]

        def entry(position, status):
            query_sum, totals_now = status
            target_device = kv_index[query_tile_index, position]
            query_gradient, pairwise_gradient = pairwise_terms(query_row_block, gradient_rows, row_norm_block, delta_row_block, pairwise_tiles[target_device], target_device == query_tile_index, KEY_VALUE_HEADS)
            return query_sum + query_gradient, totals_now.at[target_device].add(pairwise_gradient)

        start_offset = (jnp.zeros((TILE_TOKENS, KEY_VALUE_HEADS, query_group, HEAD_SIZE), jnp.float32), running_totals)
        query_sum, running_totals = lax.fori_loop(0, counts[query_tile_index], entry, start_offset)
        return running_totals, query_sum.astype(jnp.bfloat16)

    initial_carry = jnp.zeros((SEQUENCE_TILES, TILE_TOKENS, KEY_VALUE_HEADS * 2 * HEAD_SIZE), jnp.float32)
    running_totals, query_grads = lax.scan(tile_step, initial_carry, jnp.arange(SEQUENCE_TILES, dtype=jnp.int32))
    pairwise_output = running_totals.astype(jnp.bfloat16).reshape(SEQUENCE_TOKENS, KEY_VALUE_HEADS, 2 * HEAD_SIZE)
    grad_queries = query_grads.reshape(SEQUENCE_TOKENS, QUERY_HEADS * HEAD_SIZE)
    key_gradient = pairwise_output[:, :, :HEAD_SIZE].reshape(SEQUENCE_TOKENS, KEY_VALUE_HEADS * HEAD_SIZE)
    value_gradient = pairwise_output[:, :, HEAD_SIZE:].reshape(SEQUENCE_TOKENS, KEY_VALUE_HEADS * HEAD_SIZE)
    return (grad_queries, key_gradient, value_gradient)
```

```python
import functools
import math

import jax
import jax.numpy as jnp
from jax import lax
from jax.experimental import pallas as pl
from jax.experimental.pallas import tpu as pltpu
from jax.sharding import PartitionSpec as P

QUERY_HEADS = 64
KEY_VALUE_HEADS = 8
HEAD_SIZE = 128
TILE = 128
GROUP = QUERY_HEADS // KEY_VALUE_HEADS
TILES = 4
NZ = 16
NY = 4
NH = 8
ROWS = 64
WIDE = GROUP * HEAD_SIZE
UP = NZ // 2
DOWN = NZ - 1 - UP
SCALE = HEAD_SIZE ** (-0.5)
LOG2E = math.log2(math.e)
MESH = pl.DeviceIdType.MESH
F32 = jnp.float32
BF16 = jnp.bfloat16


def position():
    ctx = lax.axis_index("ctx")
    return lax.axis_index("head"), ctx // NY, lax.rem(ctx, NY)


def entry_barrier(h, z, y):
    barrier = pltpu.get_barrier_semaphore()

    def signal(**where):
        pl.semaphore_signal(barrier, inc=1, device_id=where, device_id_type=MESH)

    for d in range(1, NH):
        signal(head=lax.rem(h + d, NH))
    for d in range(1, NY):
        signal(ctx=z * NY + lax.rem(y + d, NY))
    signal(ctx=lax.rem(z + 1, NZ) * NY + y)
    signal(ctx=lax.rem(z + NZ - 1, NZ) * NY + y)
    pl.semaphore_wait(barrier, NH + NY)


def make_selection(z, y, lists_ref, sel_ref):
    slot = lax.broadcasted_iota(jnp.int32, (NZ, 128), 0)
    plane = lax.rem(z - slot + NZ, NZ)
    for dy in range(NY):
        node = z * NY + lax.rem(y + dy, NY)
        entries = lists_ref[pl.ds(node, 1), :]
        match = (entries >> 2) == plane * NY + y
        found = jnp.max(jnp.where(match, entries & 3, -1), axis=1, keepdims=True)
        sel_ref[dy] = jnp.broadcast_to(found, (NZ, 128))


def forward_kernel(
    q_ref, do_ref, k_ref, v_ref, st_ref, lists_ref,
    qh_ref, doh_ref, sth_ref, kv_ref,
    gath, picked, sel,
    x_send, x_recv, local, u_send, u_recv, d_send, d_recv, y_send, y_recv, out_sem,
):
    h, z, y = position()
    above = lax.rem(z + 1, NZ) * NY + y
    below = lax.rem(z + NZ - 1, NZ) * NY + y
    entry_barrier(h, z, y)

    def columns(owner, width):
        return pl.ds(pl.multiple_of(owner * width, width), width)

    half = pl.ds(pl.multiple_of(lax.rem(h, 2) * ROWS, ROWS), ROWS)
    mine = pl.ds(pl.multiple_of(h * ROWS, ROWS), ROWS)

    def head_parts(owner):
        return (
            (k_ref.at[:, columns(owner, HEAD_SIZE)], gath.at[0, h // 2, half, pl.ds(0, HEAD_SIZE)]),
            (v_ref.at[:, columns(owner, HEAD_SIZE)], gath.at[0, h // 2, half, pl.ds(HEAD_SIZE, HEAD_SIZE)]),
            (q_ref.at[:, columns(owner, WIDE)], qh_ref.at[mine, :]),
            (do_ref.at[:, columns(owner, WIDE)], doh_ref.at[mine, :]),
            (st_ref.at[owner], sth_ref.at[h]),
        )

    def head_copy(d, part):
        owner = lax.rem(h + d, NH)
        src, dst = head_parts(owner)[part]
        return pltpu.make_async_remote_copy(
            src_ref=src, dst_ref=dst, send_sem=x_send.at[part, d - 1], recv_sem=x_recv.at[part, d - 1],
            device_id={"head": owner}, device_id_type=MESH,
        )

    def own_copy(part):
        src, dst = head_parts(h)[part]
        return pltpu.make_async_copy(src, dst, local.at[part])

    def up_copy(k, c):
        return pltpu.make_async_remote_copy(
            src_ref=gath.at[k, c], dst_ref=gath.at[k + 1, c], send_sem=u_send.at[k, c], recv_sem=u_recv.at[k, c],
            device_id={"ctx": above}, device_id_type=MESH,
        )

    def down_copy(k, c):
        return pltpu.make_async_remote_copy(
            src_ref=gath.at[lax.rem(NZ - k, NZ), c], dst_ref=gath.at[NZ - 1 - k, c],
            send_sem=d_send.at[k, c], recv_sem=d_recv.at[k, c],
            device_id={"ctx": below}, device_id_type=MESH,
        )

    def across_copy(s, dy):
        return pltpu.make_async_remote_copy(
            src_ref=picked.at[s, dy], dst_ref=kv_ref.at[TILES + s * NY + dy],
            send_sem=y_send.at[s, dy - 1], recv_sem=y_recv.at[s, dy - 1],
            device_id={"ctx": z * NY + lax.rem(y + dy, NY)}, device_id_type=MESH,
        )

    def keep_copy(s):
        return pltpu.make_async_copy(picked.at[s, 0], kv_ref.at[TILES + s * NY], out_sem.at[s])

    own_tiles = pltpu.make_async_copy(gath.at[0], kv_ref.at[pl.ds(0, TILES)], out_sem.at[NZ])

    for part in (0, 1):
        for d in range(1, NH):
            head_copy(d, part).start()
        own_copy(part).start()
    make_selection(z, y, lists_ref, sel)
    for part in (0, 1):
        own_copy(part).wait()
        for d in range(1, NH):
            head_copy(d, part).wait_recv()

    def pick(s):
        for dy in range(NY):
            want = sel[dy, pl.ds(s, 1), :]
            for c in range(TILES):
                weight = (want == c).astype(F32).astype(BF16)
                weight = jnp.concatenate([weight, weight], axis=1)
                term = gath[s, c] * weight
                total = term if c == 0 else total + term
            picked[s, dy] = total
            if dy == 0:
                keep_copy(s).start()
            else:
                across_copy(s, dy).start()

    def ring(k, _):
        @pl.loop(0, TILES)
        def _(c):
            @pl.when(k > 0)
            def _():
                up_copy(k - 1, c).wait_recv()

            up_copy(k, c).start()

            @pl.when(k > 0)
            def _():
                down_copy(k - 1, c).wait_recv()

            @pl.when(k < DOWN)
            def _():
                down_copy(k, c).start()

        @pl.when(k == 0)
        def _():
            for part in (2, 3, 4):
                for d in range(1, NH):
                    head_copy(d, part).start()
                own_copy(part).start()
            own_tiles.start()

        pick(k)

        @pl.when(k > 0)
        def _():
            pick(NZ - k)

        return 0

    lax.fori_loop(0, UP, ring, 0)
    for c in range(TILES):
        up_copy(UP - 1, c).wait_recv()
    pick(UP)

    @pl.loop(0, NZ)
    def _(s):
        keep_copy(s).wait()
        for dy in range(1, NY):
            across_copy(s, dy).wait()

    @pl.loop(0, UP)
    def _(k):
        for c in range(TILES):
            up_copy(k, c).wait_send()

    @pl.loop(0, DOWN)
    def _(k):
        for c in range(TILES):
            down_copy(k, c).wait_send()

    own_tiles.wait()
    for part in (0, 1):
        for d in range(1, NH):
            head_copy(d, part).wait_send()
    for part in (2, 3, 4):
        own_copy(part).wait()
        for d in range(1, NH):
            head_copy(d, part).wait()


def pairs_kernel(index_ref, count_ref, q_ref, do_ref, st_ref, kv_ref, dq_ref, own_ref, slot_ref, qs, ds, total, dqt):
    h, z, y = position()
    del h
    node = z * NY + y

    @pl.loop(0, TILES + NZ * NY)
    def _(i):
        total[i] = jnp.zeros((TILE, 2 * HEAD_SIZE), F32)

    order = lax.broadcasted_iota(jnp.int32, (TILE, TILE), 0) - lax.broadcasted_iota(jnp.int32, (TILE, TILE), 1)
    order = jnp.concatenate([order, order], axis=1)
    nt = (((1,), (1,)), ((), ()))
    tn = (((0,), (0,)), ((), ()))

    @pl.loop(0, TILES)
    def _(t):
        rows = pl.ds(pl.multiple_of(t * TILE, TILE), TILE)
        for g in range(GROUP):
            qs[g * TILE : (g + 1) * TILE] = q_ref[rows, g * HEAD_SIZE : (g + 1) * HEAD_SIZE]
            ds[g * TILE : (g + 1) * TILE] = do_ref[rows, g * HEAD_SIZE : (g + 1) * HEAD_SIZE]
        dqt[...] = jnp.zeros_like(dqt)
        stats = st_ref[2 * t] + st_ref[2 * t + 1]
        query_tile = node * TILES + t

        def entry(p, _):
            tile = index_ref[query_tile, p]
            holder = tile // TILES
            slot = lax.rem(z - holder // NY + NZ, NZ) * NY + lax.rem(y - lax.rem(holder, NY) + NY, NY)
            place = jnp.where(holder == node, lax.rem(tile, TILES), TILES + slot)
            limit = jnp.where(tile == query_tile, 0, TILE)
            key = kv_ref[place, :, :HEAD_SIZE]
            value = kv_ref[place, :, HEAD_SIZE:]
            dk = jnp.zeros((TILE, HEAD_SIZE), F32)
            dv = jnp.zeros((TILE, HEAD_SIZE), F32)
            for g in range(0, GROUP, 2):
                span = slice(g * TILE, (g + 2) * TILE)
                norm = jnp.concatenate([stats[g : g + 1], stats[g + 1 : g + 2]], axis=1)
                delta = jnp.concatenate([stats[GROUP + g : GROUP + g + 1], stats[GROUP + g + 1 : GROUP + g + 2]], axis=1)
                q2 = qs[span]
                d2 = ds[span]
                scores = lax.dot_general(key, q2, nt, preferred_element_type=F32)
                weights = jnp.where(order <= limit, jnp.exp2(scores * (SCALE * LOG2E) - norm), 0.0)
                dp = lax.dot_general(value, d2, nt, preferred_element_type=F32)
                score_grad = (weights * (dp - delta)).astype(BF16)
                dv += jnp.dot(weights.astype(BF16), d2, preferred_element_type=F32)
                dk += jnp.dot(score_grad, q2, preferred_element_type=F32)
                dqt[:, span] += lax.dot_general(key, score_grad, tn, preferred_element_type=F32)
            total[place, :, :HEAD_SIZE] += dk
            total[place, :, HEAD_SIZE:] += dv
            return 0

        lax.fori_loop(0, count_ref[query_tile], entry, 0)
        for g in range(GROUP):
            part = dqt[:, g * TILE : (g + 1) * TILE] * SCALE
            dq_ref[rows, g * HEAD_SIZE : (g + 1) * HEAD_SIZE] = part.T.astype(BF16)

    for c in range(TILES):
        own_ref[c, :, :HEAD_SIZE] = total[c, :, :HEAD_SIZE] * SCALE
        own_ref[c, :, HEAD_SIZE:] = total[c, :, HEAD_SIZE:]

    @pl.loop(0, NZ * NY)
    def _(i):
        slot_ref[i, :, :HEAD_SIZE] = (total[TILES + i, :, :HEAD_SIZE] * SCALE).astype(BF16)
        slot_ref[i, :, HEAD_SIZE:] = total[TILES + i, :, HEAD_SIZE:].astype(BF16)


def backward_kernel(
    dq_ref, own_ref, slot_ref, lists_ref,
    gq_ref, gk_ref, gv_ref,
    across, up_out, up_in, down_out, down_in, done, sel,
    x_send, x_recv, local, u_send, u_recv, d_send, d_recv, y_send, y_recv,
):
    h, z, y = position()
    above = lax.rem(z + 1, NZ) * NY + y
    below = lax.rem(z + NZ - 1, NZ) * NY + y
    entry_barrier(h, z, y)

    def columns(owner, width):
        return pl.ds(pl.multiple_of(owner * width, width), width)

    def head_parts(owner):
        half = pl.ds(pl.multiple_of(lax.rem(owner, 2) * ROWS, ROWS), ROWS)
        rows = pl.ds(pl.multiple_of(owner * ROWS, ROWS), ROWS)
        return (
            (dq_ref.at[rows, :], gq_ref.at[:, columns(h, WIDE)]),
            (done.at[owner // 2, half, pl.ds(0, HEAD_SIZE)], gk_ref.at[:, columns(h, HEAD_SIZE)]),
            (done.at[owner // 2, half, pl.ds(HEAD_SIZE, HEAD_SIZE)], gv_ref.at[:, columns(h, HEAD_SIZE)]),
        )

    def head_copy(d, part):
        owner = lax.rem(h + d, NH)
        src, dst = head_parts(owner)[part]
        return pltpu.make_async_remote_copy(
            src_ref=src, dst_ref=dst, send_sem=x_send.at[part, d - 1], recv_sem=x_recv.at[part, d - 1],
            device_id={"head": owner}, device_id_type=MESH,
        )

    def own_copy(part):
        src, dst = head_parts(h)[part]
        return pltpu.make_async_copy(src, dst, local.at[part])

    def across_copy(s, dy):
        return pltpu.make_async_remote_copy(
            src_ref=slot_ref.at[s * NY + dy], dst_ref=across.at[s, dy - 1],
            send_sem=y_send.at[s, dy - 1], recv_sem=y_recv.at[s, dy - 1],
            device_id={"ctx": z * NY + lax.rem(y + NY - dy, NY)}, device_id_type=MESH,
        )

    def down_copy(k, c):
        return pltpu.make_async_remote_copy(
            src_ref=down_out.at[k, c], dst_ref=down_in.at[k, c], send_sem=d_send.at[k, c], recv_sem=d_recv.at[k, c],
            device_id={"ctx": below}, device_id_type=MESH,
        )

    def up_copy(k, c):
        return pltpu.make_async_remote_copy(
            src_ref=up_out.at[k, c], dst_ref=up_in.at[k, c], send_sem=u_send.at[k, c], recv_sem=u_recv.at[k, c],
            device_id={"ctx": above}, device_id_type=MESH,
        )

    def send_across(s):
        for dy in range(1, NY):
            across_copy(s, dy).start()

    @pl.loop(0, UP)
    def _(k):
        send_across(UP - k)

        @pl.when(k < DOWN)
        def _():
            send_across(UP + 1 + k)

    send_across(0)
    for d in range(1, NH):
        head_copy(d, 0).start()
    own_copy(0).start()
    make_selection(z, y, lists_ref, sel)

    def wait_across(s):
        for dy in range(1, NY):
            across_copy(s, dy).wait_recv()

    def asked(s, c, first):
        total = None
        for dy in range(first, NY):
            want = sel[dy, pl.ds(s, 1), :]
            weight = (want == c).astype(F32)
            weight = jnp.concatenate([weight, weight], axis=1)
            block = slot_ref[s * NY] if dy == 0 else across[s, dy - 1]
            term = block.astype(F32) * weight
            total = term if total is None else total + term
        return total

    def ring(k, _):
        wait_across(UP - k)

        @pl.when(k < DOWN)
        def _():
            wait_across(UP + 1 + k)

        @pl.loop(0, TILES)
        def _(c):
            part = asked(UP - k, c, 0)

            @pl.when(k == 0)
            def _():
                down_out[k, c] = part.astype(BF16)

            @pl.when(k > 0)
            def _():
                down_copy(k - 1, c).wait_recv()
                down_out[k, c] = (part + down_in[k - 1, c].astype(F32)).astype(BF16)

            down_copy(k, c).start()

            @pl.when(k < DOWN)
            def _():
                other = asked(UP + 1 + k, c, 0)

                @pl.when(k == 0)
                def _():
                    up_out[k, c] = other.astype(BF16)

                @pl.when(k > 0)
                def _():
                    up_copy(k - 1, c).wait_recv()
                    up_out[k, c] = (other + up_in[k - 1, c].astype(F32)).astype(BF16)

                up_copy(k, c).start()

        return 0

    lax.fori_loop(0, UP, ring, 0)
    wait_across(0)

    @pl.loop(0, TILES)
    def _(c):
        part = own_ref[c] + asked(0, c, 1)
        up_copy(DOWN - 1, c).wait_recv()
        part += up_in[DOWN - 1, c].astype(F32)
        down_copy(UP - 1, c).wait_recv()
        done[c] = (part + down_in[UP - 1, c].astype(F32)).astype(BF16)

    for part in (1, 2):
        for d in range(1, NH):
            head_copy(d, part).start()
        own_copy(part).start()

    @pl.loop(0, NZ)
    def _(s):
        for dy in range(1, NY):
            across_copy(s, dy).wait_send()

    @pl.loop(0, UP)
    def _(k):
        for c in range(TILES):
            down_copy(k, c).wait_send()

    @pl.loop(0, DOWN)
    def _(k):
        for c in range(TILES):
            up_copy(k, c).wait_send()

    for part in (0, 1, 2):
        own_copy(part).wait()
        for d in range(1, NH):
            head_copy(d, part).wait()


def any_spec():
    return pl.BlockSpec(memory_space=pl.ANY)


def vmem_spec():
    return pl.BlockSpec(memory_space=pltpu.VMEM)


def smem_spec():
    return pl.BlockSpec(memory_space=pltpu.SMEM)


def shape(dims, dtype):
    return jax.ShapeDtypeStruct(dims, dtype)


def on_device(queries, outputs, output_gradient, keys, values, log_row_norm, kv_index, counts):
    dma = pltpu.SemaphoreType.DMA
    delta = jnp.sum(
        (output_gradient.astype(F32) * outputs.astype(F32)).reshape(ROWS, QUERY_HEADS, HEAD_SIZE), axis=2
    )
    stats = jnp.concatenate(
        [(log_row_norm * LOG2E).T.reshape(NH, GROUP, ROWS), delta.T.reshape(NH, GROUP, ROWS)], axis=1
    )
    odd = lax.rem(lax.axis_index("head"), 2) == 1
    stats = jnp.concatenate([jnp.where(odd, 0.0, stats), jnp.where(odd, stats, 0.0)], axis=2)
    listed = jnp.arange(kv_index.shape[1], dtype=jnp.int32)[None, :] < counts[:, None]
    lists = jnp.where(listed, kv_index, -1).reshape(NZ * NY, -1)
    lists = jnp.pad(lists, ((0, 0), (0, 128 - lists.shape[1])), constant_values=-1)

    tile_pair = (TILE, 2 * HEAD_SIZE)
    qh, doh, sth, kv = pl.pallas_call(
        forward_kernel,
        out_shape=(
            shape((NH * ROWS, WIDE), BF16),
            shape((NH * ROWS, WIDE), BF16),
            shape((NH, 2 * GROUP, 128), F32),
            shape((TILES + NZ * NY,) + tile_pair, BF16),
        ),
        in_specs=[any_spec()] * 5 + [vmem_spec()],
        out_specs=(any_spec(),) * 4,
        scratch_shapes=[
            pltpu.VMEM((NZ, TILES) + tile_pair, BF16),
            pltpu.VMEM((NZ, NY) + tile_pair, BF16),
            pltpu.VMEM((NY, NZ, 128), jnp.int32),
            dma((5, NH - 1)), dma((5, NH - 1)), dma((5,)),
            dma((UP, TILES)), dma((UP, TILES)), dma((DOWN, TILES)), dma((DOWN, TILES)),
            dma((NZ, NY - 1)), dma((NZ, NY - 1)), dma((NZ + 1,)),
        ],
        compiler_params=pltpu.CompilerParams(collective_id=0, has_side_effects=True, vmem_limit_bytes=24 << 20),
        name="exchange_in",
    )(queries, output_gradient, keys, values, stats, lists)

    dq, own, slots = pl.pallas_call(
        pairs_kernel,
        out_shape=(
            shape((NH * ROWS, WIDE), BF16),
            shape((TILES,) + tile_pair, F32),
            shape((NZ * NY,) + tile_pair, BF16),
        ),
        in_specs=[smem_spec()] * 2 + [vmem_spec()] * 4,
        out_specs=(vmem_spec(),) * 3,
        scratch_shapes=[
            pltpu.VMEM((GROUP * TILE, HEAD_SIZE), BF16),
            pltpu.VMEM((GROUP * TILE, HEAD_SIZE), BF16),
            pltpu.VMEM((TILES + NZ * NY,) + tile_pair, F32),
            pltpu.VMEM((HEAD_SIZE, GROUP * TILE), F32),
        ],
        compiler_params=pltpu.CompilerParams(vmem_limit_bytes=48 << 20),
        name="pairs",
    )(kv_index, counts, qh, doh, sth, kv)

    return pl.pallas_call(
        backward_kernel,
        out_shape=(
            shape((ROWS, NH * WIDE), BF16),
            shape((ROWS, NH * HEAD_SIZE), BF16),
            shape((ROWS, NH * HEAD_SIZE), BF16),
        ),
        in_specs=[any_spec(), vmem_spec(), vmem_spec(), vmem_spec()],
        out_specs=(any_spec(),) * 3,
        scratch_shapes=[
            pltpu.VMEM((NZ, NY - 1) + tile_pair, BF16),
            pltpu.VMEM((DOWN, TILES) + tile_pair, BF16),
            pltpu.VMEM((DOWN, TILES) + tile_pair, BF16),
            pltpu.VMEM((UP, TILES) + tile_pair, BF16),
            pltpu.VMEM((UP, TILES) + tile_pair, BF16),
            pltpu.VMEM((TILES,) + tile_pair, BF16),
            pltpu.VMEM((NY, NZ, 128), jnp.int32),
            dma((3, NH - 1)), dma((3, NH - 1)), dma((3,)),
            dma((DOWN, TILES)), dma((DOWN, TILES)), dma((UP, TILES)), dma((UP, TILES)),
            dma((NZ, NY - 1)), dma((NZ, NY - 1)),
        ],
        compiler_params=pltpu.CompilerParams(collective_id=1, has_side_effects=True, vmem_limit_bytes=40 << 20),
        name="exchange_out",
    )(dq, own, slots, lists)


def solution(mesh):
    rows = P(("ctx", "head"), None)
    return jax.shard_map(
        on_device,
        mesh=mesh,
        in_specs=(rows,) * 6 + (P(), P()),
        out_specs=(rows,) * 3,
        check_vma=False,
    )
```

```python
import math

import jax
import jax.numpy as jnp
from jax import lax
from jax.experimental import pallas as pl
from jax.experimental.pallas import tpu as pltpu
from jax.sharding import PartitionSpec as P

QUERY_HEADS = 64
KEY_VALUE_HEADS = 8
HEAD_SIZE = 128
TILE = 128
GROUP = QUERY_HEADS // KEY_VALUE_HEADS
TILES = 4
ENTRIES = 10
PAIRS = TILES * ENTRIES
NZ = 16
NY = 4
NH = 8
HOPS = NZ // 2
CHUNK = TILES // 2
ROWS = 64
WIDE = GROUP * HEAD_SIZE
PLACES = TILES + NZ * NY
SCALE = HEAD_SIZE ** (-0.5)
LOG2E = math.log2(math.e)
MESH = pl.DeviceIdType.MESH
F32 = jnp.float32
BF16 = jnp.bfloat16
NT = (((1,), (1,)), ((), ()))
TN = (((0,), (0,)), ((), ()))

K, V, Q, DO, ST, GQ, GV, GK = range(8)


def kernel(
    q_ref, o_ref, do_ref, k_ref, v_ref, norm_ref, lists_ref, meta_ref,
    gq_ref, gk_ref, gv_ref,
    k_ring, v_ring, k_all, v_all, picked, q_all, do_all, o_own, do_own, norm_t, st_out, st_all, sel,
    weights, dv_pairs, dk_pairs, dq_t, dq_out, terms, dv_across, dk_across, down_out, up_out,
    dv_down, dv_up, dk_down, dk_up, dv_done, dk_done,
    x_send, x_recv, local, own_sem,
    u_send, u_recv, d_send, d_recv, y_send, y_recv,
    bu_send, bu_recv, bd_send, bd_recv, by_send, by_recv,
):
    ctx = lax.axis_index("ctx")
    h, z, y = lax.axis_index("head"), ctx // NY, lax.rem(ctx, NY)
    above = lax.rem(z + 1, NZ) * NY + y
    below = lax.rem(z + NZ - 1, NZ) * NY + y

    barrier = pltpu.get_barrier_semaphore()

    def greet(**where):
        pl.semaphore_signal(barrier, inc=1, device_id=where, device_id_type=MESH)

    for d in range(1, NH):
        greet(head=lax.rem(h + d, NH))
    for d in range(1, NY):
        greet(ctx=z * NY + lax.rem(y + d, NY))
    greet(ctx=above)
    greet(ctx=below)

    own_load = [
        pltpu.make_async_copy(o_ref, o_own, own_sem.at[0]),
        pltpu.make_async_copy(do_ref, do_own, own_sem.at[1]),
    ]
    for copy in own_load:
        copy.start()
    pl.semaphore_wait(barrier, NH + NY)

    def columns(owner, width):
        return pl.ds(pl.multiple_of(owner * width, width), width)

    def half(owner):
        return pl.ds(pl.multiple_of(lax.rem(owner, 2) * ROWS, ROWS), ROWS)

    def rows_of(owner):
        return pl.ds(pl.multiple_of(owner * ROWS, ROWS), ROWS)

    def head_ends(part, owner, d):
        if part == K:
            return k_ref.at[:, columns(owner, HEAD_SIZE)], k_ring.at[0, h // 2, half(h), :]
        if part == V:
            return v_ref.at[:, columns(owner, HEAD_SIZE)], v_ring.at[0, h // 2, half(h), :]
        if part == Q:
            return q_ref.at[:, columns(owner, WIDE)], q_all.at[rows_of(h), :]
        if part == DO:
            return do_ref.at[:, columns(owner, WIDE)], do_all.at[rows_of(h), :]
        if part == ST:
            return st_out.at[d], st_all.at[h]
        if part == GQ:
            return dq_out.at[rows_of(owner), :], gq_ref.at[:, columns(h, WIDE)]
        if part == GV:
            return dv_done.at[owner // 2, half(owner), :], gv_ref.at[:, columns(h, HEAD_SIZE)]
        return dk_done.at[owner // 2, half(owner), :], gk_ref.at[:, columns(h, HEAD_SIZE)]

    def head_copy(part, d):
        owner = lax.rem(h + d, NH)
        src, dst = head_ends(part, owner, d)
        return pltpu.make_async_remote_copy(
            src_ref=src, dst_ref=dst, send_sem=x_send.at[part, d - 1], recv_sem=x_recv.at[part, d - 1],
            device_id={"head": owner}, device_id_type=MESH,
        )

    def own_copy(part):
        src, dst = head_ends(part, h, 0)
        return pltpu.make_async_copy(src, dst, local.at[part])

    def head_start(part):
        for d in range(1, NH):
            head_copy(part, d).start()
        own_copy(part).start()

    def head_arrived(part):
        own_copy(part).wait()
        for d in range(1, NH):
            head_copy(part, d).wait_recv()

    def head_sent(part):
        for d in range(1, NH):
            head_copy(part, d).wait_send()

    ring_of, all_of = (k_ring, v_ring), (k_all, v_all)

    def tiles(c):
        return pl.ds(c * CHUNK, CHUNK)

    def up_copy(w, j, c):
        ring = ring_of[w]
        return pltpu.make_async_remote_copy(
            src_ref=ring.at[j, tiles(c)], dst_ref=ring.at[j + 1, tiles(c)],
            send_sem=u_send.at[w, j, c], recv_sem=u_recv.at[w, j, c],
            device_id={"ctx": above}, device_id_type=MESH,
        )

    def down_copy(w, j, c):
        ring = ring_of[w]
        return pltpu.make_async_remote_copy(
            src_ref=ring.at[lax.rem(NZ - j, NZ), tiles(c)], dst_ref=ring.at[NZ - 1 - j, tiles(c)],
            send_sem=d_send.at[w, j, c], recv_sem=d_recv.at[w, j, c],
            device_id={"ctx": below}, device_id_type=MESH,
        )

    def across_copy(w, s, dy):
        return pltpu.make_async_remote_copy(
            src_ref=picked.at[w, s, dy - 1], dst_ref=all_of[w].at[TILES + s * NY + dy],
            send_sem=y_send.at[w, s, dy - 1], recv_sem=y_recv.at[w, s, dy - 1],
            device_id={"ctx": z * NY + lax.rem(y + dy, NY)}, device_id_type=MESH,
        )

    def pick(w, s):
        ring = ring_of[w]
        for dy in range(NY):
            want = sel[dy, pl.ds(s, 1), :]
            for c in range(TILES):
                term = ring[s, c] * (want == c).astype(F32).astype(BF16)
                total = term if c == 0 else total + term
            if dy == 0:
                all_of[w][TILES + s * NY] = total
            else:
                picked[w, s, dy - 1] = total
                across_copy(w, s, dy).start()

    def gather(w, beside):
        def step(j, _):
            for c in range(2):

                @pl.when(j > 0)
                def _():
                    up_copy(w, j - 1, c).wait_recv()

                if c == 0:
                    up_copy(w, j, c).start()
                else:

                    @pl.when(j < HOPS - 1)
                    def _():
                        up_copy(w, j, c).start()

                @pl.when(j > 0)
                def _():
                    down_copy(w, j - 1, c).wait_recv()

                if c == 1:
                    down_copy(w, j, c).start()
                else:

                    @pl.when(j < HOPS - 1)
                    def _():
                        down_copy(w, j, c).start()

                if c == 1:
                    pick(w, j)

                    @pl.when(j > 0)
                    def _():
                        pick(w, NZ - j)

                beside(j, c)
            return 0

        lax.fori_loop(0, HOPS, step, 0)

    def gather_end(w):
        up_copy(w, HOPS - 1, 0).wait_recv()
        down_copy(w, HOPS - 1, 1).wait_recv()
        pick(w, HOPS)

    def gathered(w):
        @pl.loop(0, NZ)
        def _(s):
            for dy in range(1, NY):
                across_copy(w, s, dy).wait_recv()

    order = lax.broadcasted_iota(jnp.int32, (TILE, TILE), 0) - lax.broadcasted_iota(jnp.int32, (TILE, TILE), 1)
    order = jnp.concatenate([order, order], axis=1)

    def two_heads(ref, t, g):
        rows = pl.ds(pl.multiple_of(t * TILE, TILE), TILE)
        return jnp.concatenate(
            [ref[rows, g * HEAD_SIZE : (g + 1) * HEAD_SIZE], ref[rows, (g + 1) * HEAD_SIZE : (g + 2) * HEAD_SIZE]],
            axis=0,
        )

    def stat_rows(t, g):
        both = st_all[2 * t] + st_all[2 * t + 1]
        return jnp.concatenate([both[g : g + 1], both[g + 1 : g + 2]], axis=1)

    def first_half(e):
        t = e // ENTRIES
        key = k_all[meta_ref[0, e]]
        limit = meta_ref[0, PAIRS + e]
        dv = jnp.zeros((TILE, HEAD_SIZE), F32)
        for g in range(0, GROUP, 2):
            scores = lax.dot_general(key, two_heads(q_all, t, g), NT, preferred_element_type=F32)
            part = jnp.where(order <= limit, jnp.exp2(scores * (SCALE * LOG2E) - stat_rows(t, g)), 0.0)
            weights[e, :, g * TILE : (g + 2) * TILE] = part
            dv += jnp.dot(part.astype(BF16), two_heads(do_all, t, g), preferred_element_type=F32)
        dv_pairs[e] = dv

    def second_half(e):
        t = e // ENTRIES
        place = meta_ref[0, e]
        key = k_all[place]
        value = v_all[place]
        dk = jnp.zeros((TILE, HEAD_SIZE), F32)
        for g in range(0, GROUP, 2):
            span = slice(g * TILE, (g + 2) * TILE)
            dp = lax.dot_general(value, two_heads(do_all, t, g), NT, preferred_element_type=F32)
            score_grad = (weights[e, :, span] * (dp - stat_rows(t, GROUP + g))).astype(BF16)
            dk += jnp.dot(score_grad, two_heads(q_all, t, g), preferred_element_type=F32)
            dq_t[t, :, span] += lax.dot_general(key, score_grad, TN, preferred_element_type=F32)
        dk_pairs[e] = dk * SCALE

    pairs_of, cross_of, done_of = (dk_pairs, dv_pairs), (dk_across, dv_across), (dk_done, dv_done)
    down_of, up_of = (dk_down, dv_down), (dk_up, dv_up)

    def cross_back(w, s, dy):
        return pltpu.make_async_remote_copy(
            src_ref=terms.at[w, s, dy], dst_ref=cross_of[w].at[s, dy - 1],
            send_sem=by_send.at[w, s, dy - 1], recv_sem=by_recv.at[w, s, dy - 1],
            device_id={"ctx": z * NY + lax.rem(y + NY - dy, NY)}, device_id_type=MESH,
        )

    def down_back(w, j, c):
        return pltpu.make_async_remote_copy(
            src_ref=down_out.at[w, j, tiles(c)], dst_ref=down_of[w].at[j, tiles(c)],
            send_sem=bd_send.at[w, j, c], recv_sem=bd_recv.at[w, j, c],
            device_id={"ctx": below}, device_id_type=MESH,
        )

    def up_back(w, j, c):
        return pltpu.make_async_remote_copy(
            src_ref=up_out.at[w, j, tiles(c)], dst_ref=up_of[w].at[j, tiles(c)],
            send_sem=bu_send.at[w, j, c], recv_sem=bu_recv.at[w, j, c],
            device_id={"ctx": above}, device_id_type=MESH,
        )

    def place_sum(w, place):
        for t in range(TILES):
            term = pairs_of[w][meta_ref[0, 2 * PAIRS + t * PLACES + place]]
            total = term if t == 0 else total + term
        return total

    def give(w, s):
        for dy in range(NY):
            terms[w, s, dy] = place_sum(w, TILES + s * NY + dy).astype(BF16)
            if dy > 0:
                cross_back(w, s, dy).start()

    def taken(w, s):
        for dy in range(1, NY):
            cross_back(w, s, dy).wait_recv()

    def asked(w, s, c, first):
        total = None
        for dy in range(first, NY):
            weight = (sel[dy, pl.ds(s, 1), :] == c).astype(F32)
            block = terms[w, s, 0] if dy == 0 else cross_of[w][s, dy - 1]
            term = block.astype(F32) * weight
            total = term if total is None else total + term
        return total

    def reduce_start(w):
        for s in (8, 7, 9, 6, 10):
            give(w, s)
        for c in range(CHUNK):
            down_of[w][0, CHUNK + c] = jnp.zeros((TILE, HEAD_SIZE), BF16)
            up_of[w][0, c] = jnp.zeros((TILE, HEAD_SIZE), BF16)

    def hop(w, j, c, out, into, slot, copy, first):
        if c == first:

            @pl.when(j == 0)
            def _():
                for i in range(c * CHUNK, (c + 1) * CHUNK):
                    out[w, 0, i] = asked(w, HOPS, i, 0).astype(BF16)
                copy(w, j, c).start()

            @pl.when(j > 0)
            def _():
                copy(w, j - 1, c).wait_recv()

        else:

            @pl.when(j > 1)
            def _():
                copy(w, j - 1, c).wait_recv()

        @pl.when(j > 0)
        def _():
            for i in range(c * CHUNK, (c + 1) * CHUNK):
                out[w, j, i] = (asked(w, slot, i, 0) + into[j - 1, i].astype(F32)).astype(BF16)
            copy(w, j, c).start()

    def reduce_ring(w, beside):
        def step(j, _):
            taken(w, HOPS - j)

            @pl.when(j > 0)
            def _():
                taken(w, HOPS + j)

            for c in range(2):
                hop(w, j, c, down_out, down_of[w], HOPS - j, down_back, 0)
                hop(w, j, c, up_out, up_of[w], HOPS + j, up_back, 1)
                if c == 1:

                    @pl.when(j < HOPS - 2)
                    def _():
                        give(w, HOPS - 3 - j)

                    @pl.when(j < HOPS - 3)
                    def _():
                        give(w, HOPS + 3 + j)

                beside(j, c)
            return 0

        lax.fori_loop(0, HOPS, step, 0)

    def reduce_end(w):
        taken(w, 0)
        for i in range(TILES):
            c = i // CHUNK
            part = place_sum(w, i) + asked(w, 0, i, 1)
            if i % CHUNK == 0:
                down_back(w, HOPS - 1, c).wait_recv()
                up_back(w, HOPS - 1, c).wait_recv()
            part += down_of[w][HOPS - 1, i].astype(F32)
            part += up_of[w][HOPS - 1, i].astype(F32)
            done_of[w][i] = part.astype(BF16)

    head_start(K)
    head_start(V)
    slot = lax.broadcasted_iota(jnp.int32, (NZ, 128), 0)
    plane = lax.rem(z - slot + NZ, NZ)
    for dy in range(NY):
        node = z * NY + lax.rem(y + dy, NY)
        entries = lists_ref[pl.ds(node, 1), :]
        match = (entries >> 2) == plane * NY + y
        found = jnp.max(jnp.where(match, entries & 3, -1), axis=1, keepdims=True)
        sel[dy] = jnp.broadcast_to(found, (NZ, 128))
    head_arrived(K)

    lane = lax.broadcasted_iota(jnp.int32, (ROWS, 128), 1)
    keep = (lax.broadcasted_iota(jnp.int32, (GROUP, 128), 1) >= ROWS) == (lax.rem(h, 2) == 1)

    def beside_keys(j, c):
        if c == 0:

            @pl.when(j == 0)
            def _():
                head_start(Q)
                head_start(DO)

        else:

            @pl.when(j == 0)
            def _():
                for copy in own_load:
                    copy.wait()
                block = jnp.concatenate([norm_ref[...], jnp.zeros((ROWS, ROWS), F32)], axis=1) * LOG2E
                norm_t[...] = jnp.concatenate([block, block], axis=0).T
                for i in range(TILES):
                    k_all[i] = k_ring[0, i]
                    dq_t[i] = jnp.zeros((HEAD_SIZE, GROUP * TILE), F32)
                dv_pairs[PAIRS] = jnp.zeros((TILE, HEAD_SIZE), F32)
                dk_pairs[PAIRS] = jnp.zeros((TILE, HEAD_SIZE), F32)

            owner = lax.rem(h + j, NH)
            cols = columns(owner, WIDE)
            product = do_own[:, cols].astype(F32) * o_own[:, cols].astype(F32)
            block = jnp.zeros((ROWS, 128), F32)
            for g in range(GROUP):
                delta = jnp.sum(product[:, g * HEAD_SIZE : (g + 1) * HEAD_SIZE], axis=1, keepdims=True)
                block = jnp.where(lane == g, delta, block)
            turned = jnp.concatenate([block, block], axis=0).T
            norms = norm_t[pl.ds(pl.multiple_of(owner * GROUP, GROUP), GROUP), :]
            st_out[j, :GROUP] = jnp.where(keep, norms, 0.0)
            st_out[j, GROUP:] = jnp.where(keep, turned[:GROUP], 0.0)

            @pl.when(j > 0)
            def _():
                head_copy(ST, j).start()

            @pl.when(j == 0)
            def _():
                own_copy(ST).start()

    gather(0, beside_keys)
    gather_end(0)

    per_step = 6

    def beside_values(j, c):
        if c == 0:

            @pl.when(j == 0)
            def _():
                for i in range(TILES):
                    v_all[i] = v_ring[0, i]

            @pl.when(j == 1)
            def _():
                for part in (Q, DO, ST):
                    head_arrived(part)
                gathered(0)

        @pl.loop(0, per_step // 2)
        def _(i):
            e = (j - 1) * per_step + c * (per_step // 2) + i

            @pl.when((j > 0) & (e < PAIRS))
            def _():
                first_half(e)

    head_arrived(V)
    gather(1, beside_values)
    gather_end(1)

    reduce_start(1)
    gathered(1)

    def beside_dv(j, c):
        @pl.loop(0, 3 - c)
        def _(i):
            second_half(j * 5 + c * 3 + i)

    reduce_ring(1, beside_dv)
    reduce_start(0)
    reduce_end(1)
    head_start(GV)

    def beside_dk(j, c):
        if c == 1:

            @pl.when(j < TILES)
            def _():
                rows = pl.ds(pl.multiple_of(j * TILE, TILE), TILE)
                for g in range(GROUP):
                    part = dq_t[j, :, g * TILE : (g + 1) * TILE] * SCALE
                    dq_out[rows, g * HEAD_SIZE : (g + 1) * HEAD_SIZE] = part.T.astype(BF16)

            @pl.when(j == TILES - 1)
            def _():
                head_start(GQ)

    reduce_ring(0, beside_dk)
    reduce_end(0)
    head_start(GK)

    for w in range(2):

        @pl.loop(0, NZ)
        def _(s, w=w):
            for dy in range(1, NY):
                across_copy(w, s, dy).wait_send()
                cross_back(w, s, dy).wait_send()

        for j in range(HOPS):
            for c in range(2):
                if j < HOPS - 1 or c == 0:
                    up_copy(w, j, c).wait_send()
                if j < HOPS - 1 or c == 1:
                    down_copy(w, j, c).wait_send()
                if j > 0 or c == 0:
                    down_back(w, j, c).wait_send()
                if j > 0 or c == 1:
                    up_back(w, j, c).wait_send()

    for part in (GV, GQ, GK):
        head_arrived(part)
    for part in range(8):
        head_sent(part)


def any_spec():
    return pl.BlockSpec(memory_space=pl.ANY)


def shape(dims, dtype):
    return jax.ShapeDtypeStruct(dims, dtype)


def on_device(queries, outputs, output_gradient, keys, values, log_row_norm, kv_index, counts):
    dma = pltpu.SemaphoreType.DMA
    vmem = pltpu.VMEM
    listed = jnp.arange(ENTRIES, dtype=jnp.int32)[None, :] < counts[:, None]
    lists = jnp.where(listed, kv_index, -1).reshape(NZ * NY, PAIRS)
    padded = jnp.pad(lists, ((0, 0), (0, 128 - PAIRS)), constant_values=-1)

    node = lax.axis_index("ctx")
    tile = lax.dynamic_index_in_dim(lists, node, 0, keepdims=False)
    holder = tile // TILES
    slot = ((node // NY - holder // NY) % NZ) * NY + (node - holder) % NY
    place = jnp.where(holder == node, tile % TILES, TILES + slot)
    place = jnp.where(tile < 0, 0, place)
    number = jnp.arange(PAIRS, dtype=jnp.int32)
    limit = jnp.where(tile == node * TILES + number // ENTRIES, 0, TILE)
    limit = jnp.where(tile < 0, -TILE, limit)
    match = (place.reshape(TILES, 1, ENTRIES) == jnp.arange(PLACES, dtype=jnp.int32)[None, :, None]) & (
        tile >= 0
    ).reshape(TILES, 1, ENTRIES)
    pair = jnp.min(jnp.where(match, number.reshape(TILES, 1, ENTRIES), PAIRS), axis=2).reshape(-1)
    meta = jnp.concatenate([place, limit, pair]).reshape(1, -1)

    block = (TILE, HEAD_SIZE)
    return pl.pallas_call(
        kernel,
        out_shape=(
            shape((ROWS, NH * WIDE), BF16),
            shape((ROWS, NH * HEAD_SIZE), BF16),
            shape((ROWS, NH * HEAD_SIZE), BF16),
        ),
        in_specs=[any_spec()] * 5
        + [pl.BlockSpec(memory_space=pltpu.VMEM)] * 2
        + [pl.BlockSpec(memory_space=pltpu.SMEM)],
        out_specs=(any_spec(),) * 3,
        scratch_shapes=[
            vmem((NZ, TILES) + block, BF16), vmem((NZ, TILES) + block, BF16),
            vmem((PLACES,) + block, BF16), vmem((PLACES,) + block, BF16),
            vmem((2, NZ, NY - 1) + block, BF16),
            vmem((NH * ROWS, WIDE), BF16), vmem((NH * ROWS, WIDE), BF16),
            vmem((ROWS, NH * WIDE), BF16), vmem((ROWS, NH * WIDE), BF16),
            vmem(block, F32), vmem((NH, 2 * GROUP, 128), F32), vmem((NH, 2 * GROUP, 128), F32),
            vmem((NY, NZ, 128), jnp.int32),
            vmem((PAIRS, TILE, GROUP * TILE), F32),
            vmem((PAIRS + 1,) + block, F32), vmem((PAIRS + 1,) + block, F32),
            vmem((TILES, HEAD_SIZE, GROUP * TILE), F32), vmem((NH * ROWS, WIDE), BF16),
            vmem((2, NZ, NY) + block, BF16),
            vmem((NZ, NY - 1) + block, BF16), vmem((NZ, NY - 1) + block, BF16),
            vmem((2, HOPS, TILES) + block, BF16), vmem((2, HOPS, TILES) + block, BF16),
            vmem((HOPS, TILES) + block, BF16), vmem((HOPS, TILES) + block, BF16),
            vmem((HOPS, TILES) + block, BF16), vmem((HOPS, TILES) + block, BF16),
            vmem((TILES,) + block, BF16), vmem((TILES,) + block, BF16),
            dma((8, NH - 1)), dma((8, NH - 1)), dma((8,)), dma((2,)),
            dma((2, HOPS, 2)), dma((2, HOPS, 2)), dma((2, HOPS, 2)), dma((2, HOPS, 2)),
            dma((2, NZ, NY - 1)), dma((2, NZ, NY - 1)),
            dma((2, HOPS, 2)), dma((2, HOPS, 2)), dma((2, HOPS, 2)), dma((2, HOPS, 2)),
            dma((2, NZ, NY - 1)), dma((2, NZ, NY - 1)),
        ],
        compiler_params=pltpu.CompilerParams(collective_id=0, has_side_effects=True, vmem_limit_bytes=63 << 20),
        cost_estimate=pl.CostEstimate(flops=6_710_886_400, bytes_accessed=12 << 20, transcendentals=5_242_880),
        name="attention_backward",
    )(queries, outputs, output_gradient, keys, values, log_row_norm, padded, meta)


def solution(mesh):
    rows = P(("ctx", "head"), None)
    return jax.shard_map(
        on_device,
        mesh=mesh,
        in_specs=(rows,) * 6 + (P(), P()),
        out_specs=(rows,) * 3,
        check_vma=False,
    )
```

```python
import math

import jax
import jax.numpy as jnp
from jax import lax
from jax.experimental import pallas as pl
from jax.experimental.pallas import tpu as pltpu
from jax.sharding import PartitionSpec as P

QUERY_HEADS = 64
KEY_VALUE_HEADS = 8
HEAD_SIZE = 128
TILE = 128
GROUP = QUERY_HEADS // KEY_VALUE_HEADS
TILES = 4
ENTRIES = 10
PAIRS = TILES * ENTRIES
NZ = 16
NY = 4
NH = 8
HOPS = NZ // 2
PLACES = TILES + (HOPS + 1) * NY * 2
LAG = 2
BACK_LAG = 3
PER_HOP = -(-PAIRS // 2 // BACK_LAG)
CHUNK = TILES // 2
ROWS = 64
WIDE = GROUP * HEAD_SIZE
SCALE = HEAD_SIZE ** (-0.5)
LOG2E = math.log2(math.e)
MESH = pl.DeviceIdType.MESH
F32 = jnp.float32
BF16 = jnp.bfloat16
NT = (((1,), (1,)), ((), ()))
TN = (((0,), (0,)), ((), ()))

K, V, Q, DO, ST, GQ, GV, GK = range(8)


def kernel(
    q_ref, o_ref, do_ref, k_ref, v_ref, norm_ref, lists_ref, meta_ref,
    gq_ref, gk_ref, gv_ref,
    k_ring, v_ring, k_all, v_all, picked, q_all, do_all, o_own, do_own, norm_t, st_out, st_all, sel,
    weights, dv_pairs, dk_pairs, dq_t, dq_out, terms, dv_across, dk_across, down_out, up_out,
    dv_down, dv_up, dk_down, dk_up, dv_done, dk_done,
    x_send, x_recv, local, own_sem,
    u_send, u_recv, d_send, d_recv, y_send, y_recv,
    bu_send, bu_recv, bd_send, bd_recv, by_send, by_recv,
):
    ctx = lax.axis_index("ctx")
    h, z, y = lax.axis_index("head"), ctx // NY, lax.rem(ctx, NY)
    above = lax.rem(z + 1, NZ) * NY + y
    below = lax.rem(z + NZ - 1, NZ) * NY + y

    barrier = pltpu.get_barrier_semaphore()

    def greet(**where):
        pl.semaphore_signal(barrier, inc=1, device_id=where, device_id_type=MESH)

    for d in range(1, NH):
        greet(head=lax.rem(h + d, NH))
    for d in range(1, NY):
        greet(ctx=z * NY + lax.rem(y + d, NY))
    greet(ctx=above)
    greet(ctx=below)

    own_load = [
        pltpu.make_async_copy(o_ref, o_own, own_sem.at[0]),
        pltpu.make_async_copy(do_ref, do_own, own_sem.at[1]),
    ]
    for copy in own_load:
        copy.start()
    pl.semaphore_wait(barrier, NH + NY)

    def columns(owner, width):
        return pl.ds(pl.multiple_of(owner * width, width), width)

    def half(owner):
        return pl.ds(pl.multiple_of(lax.rem(owner, 2) * ROWS, ROWS), ROWS)

    def rows_of(owner):
        return pl.ds(pl.multiple_of(owner * ROWS, ROWS), ROWS)

    def head_ends(part, owner, d):
        if part == K:
            return k_ref.at[:, columns(owner, HEAD_SIZE)], k_ring.at[0, h // 2, half(h), :]
        if part == V:
            return v_ref.at[:, columns(owner, HEAD_SIZE)], v_ring.at[0, h // 2, half(h), :]
        if part == Q:
            return q_ref.at[:, columns(owner, WIDE)], q_all.at[rows_of(h), :]
        if part == DO:
            return do_ref.at[:, columns(owner, WIDE)], do_all.at[rows_of(h), :]
        if part == ST:
            return st_out.at[d], st_all.at[h]
        if part == GQ:
            return dq_out.at[rows_of(owner), :], gq_ref.at[:, columns(h, WIDE)]
        if part == GV:
            return dv_done.at[owner // 2, half(owner), :], gv_ref.at[:, columns(h, HEAD_SIZE)]
        return dk_done.at[owner // 2, half(owner), :], gk_ref.at[:, columns(h, HEAD_SIZE)]

    def head_copy(part, d):
        owner = lax.rem(h + d, NH)
        src, dst = head_ends(part, owner, d)
        return pltpu.make_async_remote_copy(
            src_ref=src, dst_ref=dst, send_sem=x_send.at[part, d - 1], recv_sem=x_recv.at[part, d - 1],
            device_id={"head": owner}, device_id_type=MESH,
        )

    def own_copy(part):
        src, dst = head_ends(part, h, 0)
        return pltpu.make_async_copy(src, dst, local.at[part])

    def head_start(part):
        for d in range(1, NH):
            head_copy(part, d).start()
        own_copy(part).start()

    def head_arrived(part):
        own_copy(part).wait()
        for d in range(1, NH):
            head_copy(part, d).wait_recv()

    def head_sent(part):
        for d in range(1, NH):
            head_copy(part, d).wait_send()

    ring_of, all_of = (k_ring, v_ring), (k_all, v_all)

    def tiles(c):
        return pl.ds(c * CHUNK, CHUNK)

    def up_copy(w, j, c):
        ring = ring_of[w]
        return pltpu.make_async_remote_copy(
            src_ref=ring.at[j, tiles(c)], dst_ref=ring.at[j + 1, tiles(c)],
            send_sem=u_send.at[w, j, c], recv_sem=u_recv.at[w, j, c],
            device_id={"ctx": above}, device_id_type=MESH,
        )

    def down_copy(w, j, c):
        ring = ring_of[w]
        return pltpu.make_async_remote_copy(
            src_ref=ring.at[lax.rem(NZ - j, NZ), tiles(c)], dst_ref=ring.at[NZ - 1 - j, tiles(c)],
            send_sem=d_send.at[w, j, c], recv_sem=d_recv.at[w, j, c],
            device_id={"ctx": below}, device_id_type=MESH,
        )

    def across_copy(w, j, dy, sides):
        return pltpu.make_async_remote_copy(
            src_ref=picked.at[w, j, dy - 1, pl.ds(0, sides)],
            dst_ref=all_of[w].at[pl.ds(TILES + (j * NY + dy) * 2, sides)],
            send_sem=y_send.at[w, j, dy - 1], recv_sem=y_recv.at[w, j, dy - 1],
            device_id={"ctx": z * NY + lax.rem(y + dy, NY)}, device_id_type=MESH,
        )

    def pick(w, s, j, side):
        ring = ring_of[w]
        for dy in range(NY):
            want = sel[dy, pl.ds(s, 1), :]
            for c in range(TILES):
                term = ring[s, c] * (want == c).astype(F32).astype(BF16)
                total = term if c == 0 else total + term
            if dy == 0:
                all_of[w][TILES + j * NY * 2 + side] = total
            else:
                picked[w, j, dy - 1, side] = total

    def picks(w, j):
        pick(w, j, j, 0)

        @pl.when(j > 0)
        def _():
            pick(w, NZ - j, j, 1)
            for dy in range(1, NY):
                across_copy(w, j, dy, 2).start()

        @pl.when(j == 0)
        def _():
            for dy in range(1, NY):
                across_copy(w, j, dy, 1).start()

    def serve(w, j, c):
        @pl.when(j > 0)
        def _():
            up_copy(w, j - 1, c).wait_recv()

        @pl.when((j < HOPS - 1) | (c == 0))
        def _():
            up_copy(w, j, c).start()

        @pl.when(j > 0)
        def _():
            down_copy(w, j - 1, c).wait_recv()

        @pl.when((j < HOPS - 1) | (c == 1))
        def _():
            down_copy(w, j, c).start()

    def gather_end(w):
        up_copy(w, HOPS - 1, 0).wait_recv()
        down_copy(w, HOPS - 1, 1).wait_recv()
        pick(w, HOPS, HOPS, 0)
        for dy in range(1, NY):
            across_copy(w, HOPS, dy, 1).start()

    def gathered(w):
        @pl.loop(1, HOPS)
        def _(j):
            for dy in range(1, NY):
                across_copy(w, j, dy, 2).wait_recv()

        for j in (0, HOPS):
            for dy in range(1, NY):
                across_copy(w, j, dy, 1).wait_recv()

    order = lax.broadcasted_iota(jnp.int32, (TILE, GROUP * TILE), 0) - lax.rem(
        lax.broadcasted_iota(jnp.int32, (TILE, GROUP * TILE), 1), TILE
    )

    def all_heads(ref, t):
        rows = pl.ds(pl.multiple_of(t * TILE, TILE), TILE)
        return jnp.concatenate([ref[rows, g * HEAD_SIZE : (g + 1) * HEAD_SIZE] for g in range(GROUP)], axis=0)

    def stat_rows(t, first):
        both = st_all[2 * t] + st_all[2 * t + 1]
        return jnp.concatenate([both[first + g : first + g + 1] for g in range(GROUP)], axis=1)

    def two_tiles(ref, e):
        return jnp.concatenate([ref[meta_ref[0, e]], ref[meta_ref[0, e + 1]]], axis=0)

    def first_half(b):
        e = 2 * b
        t = e // ENTRIES
        scores = lax.dot_general(two_tiles(k_all, e), all_heads(q_all, t), NT, preferred_element_type=F32)
        full = jnp.exp2(scores * (SCALE * LOG2E) - stat_rows(t, 0))
        parts = []
        for i in range(2):
            part = jnp.where(order <= meta_ref[0, PAIRS + e + i], full[i * TILE : (i + 1) * TILE], 0.0)
            weights[e + i] = part
            parts.append(part.astype(BF16))
        dv = jnp.dot(jnp.concatenate(parts, axis=0), all_heads(do_all, t), preferred_element_type=F32)
        for i in range(2):
            dv_pairs[e + i] = dv[i * TILE : (i + 1) * TILE]

    def second_half(b):
        e = 2 * b
        t = e // ENTRIES
        dp = lax.dot_general(two_tiles(v_all, e), all_heads(do_all, t), NT, preferred_element_type=F32)
        delta = stat_rows(t, GROUP)
        parts = [(weights[e + i] * (dp[i * TILE : (i + 1) * TILE] - delta)).astype(BF16) for i in range(2)]
        score_grad = jnp.concatenate(parts, axis=0)
        dk = jnp.dot(score_grad, all_heads(q_all, t), preferred_element_type=F32) * SCALE
        for i in range(2):
            dk_pairs[e + i] = dk[i * TILE : (i + 1) * TILE]
        dq_t[t] += lax.dot_general(two_tiles(k_all, e), score_grad, TN, preferred_element_type=F32)

    pairs_of, cross_of, done_of = (dk_pairs, dv_pairs), (dk_across, dv_across), (dk_done, dv_done)
    down_of, up_of = (dk_down, dv_down), (dk_up, dv_up)

    def cross_back(w, j, dy, sides):
        return pltpu.make_async_remote_copy(
            src_ref=terms.at[w, j, dy, pl.ds(0, sides)], dst_ref=cross_of[w].at[j, dy - 1, pl.ds(0, sides)],
            send_sem=by_send.at[w, j, dy - 1], recv_sem=by_recv.at[w, j, dy - 1],
            device_id={"ctx": z * NY + lax.rem(y + NY - dy, NY)}, device_id_type=MESH,
        )

    def down_back(w, j, c):
        return pltpu.make_async_remote_copy(
            src_ref=down_out.at[w, j, tiles(c)], dst_ref=down_of[w].at[j, tiles(c)],
            send_sem=bd_send.at[w, j, c], recv_sem=bd_recv.at[w, j, c],
            device_id={"ctx": below}, device_id_type=MESH,
        )

    def up_back(w, j, c):
        return pltpu.make_async_remote_copy(
            src_ref=up_out.at[w, j, tiles(c)], dst_ref=up_of[w].at[j, tiles(c)],
            send_sem=bu_send.at[w, j, c], recv_sem=bu_recv.at[w, j, c],
            device_id={"ctx": above}, device_id_type=MESH,
        )

    def place_sum(w, place):
        for t in range(TILES):
            term = pairs_of[w][meta_ref[0, 2 * PAIRS + t * PLACES + place]]
            total = term if t == 0 else total + term
        return total

    def give(w, j, sides):
        for dy in range(NY):
            for side in range(sides):
                terms[w, j, dy, side] = place_sum(w, TILES + (j * NY + dy) * 2 + side).astype(BF16)
            if dy > 0:
                cross_back(w, j, dy, sides).start()

    def taken(w, j, sides):
        for dy in range(1, NY):
            cross_back(w, j, dy, sides).wait_recv()

    def asked(w, s, j, side, c, first):
        total = None
        for dy in range(first, NY):
            weight = (sel[dy, pl.ds(s, 1), :] == c).astype(F32)
            block = terms[w, j, 0, side] if dy == 0 else cross_of[w][j, dy - 1, side]
            term = block.astype(F32) * weight
            total = term if total is None else total + term
        return total

    def reduce_start(w):
        give(w, HOPS, 1)
        for j in (HOPS - 1, HOPS - 2):
            give(w, j, 2)
        for c in range(CHUNK):
            down_of[w][0, CHUNK + c] = jnp.zeros((TILE, HEAD_SIZE), BF16)
            up_of[w][0, c] = jnp.zeros((TILE, HEAD_SIZE), BF16)

    def hop(w, j, c, out, into, side, copy, first):
        slot = HOPS + j if side == 1 else HOPS - j

        if c == first:

            @pl.when(j == 0)
            def _():
                for i in range(c * CHUNK, (c + 1) * CHUNK):
                    out[w, 0, i] = asked(w, HOPS, HOPS, 0, i, 0).astype(BF16)
                copy(w, j, c).start()

            @pl.when(j > 0)
            def _():
                copy(w, j - 1, c).wait_recv()

        else:

            @pl.when(j > 1)
            def _():
                copy(w, j - 1, c).wait_recv()

        @pl.when(j > 0)
        def _():
            for i in range(c * CHUNK, (c + 1) * CHUNK):
                part = asked(w, slot, HOPS - j, side, i, 0)
                out[w, j, i] = (part + into[j - 1, i].astype(F32)).astype(BF16)
            copy(w, j, c).start()

    def take(w, j):
        @pl.when(j == 0)
        def _():
            taken(w, HOPS - j, 1)

        @pl.when(j > 0)
        def _():
            taken(w, HOPS - j, 2)

    def hops(w, j, c):
        hop(w, j, c, down_out, down_of[w], 0, down_back, 0)
        hop(w, j, c, up_out, up_of[w], 1, up_back, 1)

    def give_next(w, j):
        @pl.when(j < HOPS - 3)
        def _():
            give(w, HOPS - 3 - j, 2)

        @pl.when(j == HOPS - 3)
        def _():
            give(w, HOPS - 3 - j, 1)

    def reduce_end(w):
        taken(w, 0, 1)
        for i in range(TILES):
            c = i // CHUNK
            part = place_sum(w, i) + asked(w, 0, 0, 0, i, 1)
            if i % CHUNK == 0:
                down_back(w, HOPS - 1, c).wait_recv()
                up_back(w, HOPS - 1, c).wait_recv()
            part += down_of[w][HOPS - 1, i].astype(F32)
            part += up_of[w][HOPS - 1, i].astype(F32)
            done_of[w][i] = part.astype(BF16)

    head_start(K)
    slot = lax.broadcasted_iota(jnp.int32, (NZ, 128), 0)
    plane = lax.rem(z - slot + NZ, NZ)
    for dy in range(NY):
        node = z * NY + lax.rem(y + dy, NY)
        entries = lists_ref[pl.ds(node, 1), :]
        match = (entries >> 2) == plane * NY + y
        found = jnp.max(jnp.where(match, entries & 3, -1), axis=1, keepdims=True)
        sel[dy] = jnp.broadcast_to(found, (NZ, 128))
    head_arrived(K)

    lane = lax.broadcasted_iota(jnp.int32, (ROWS, 128), 1)
    keep = (lax.broadcasted_iota(jnp.int32, (GROUP, 128), 1) >= ROWS) == (lax.rem(h, 2) == 1)

    def prepare(i):
        @pl.when(i == 0)
        def _():
            for copy in own_load:
                copy.wait()
            block = jnp.concatenate([norm_ref[...], jnp.zeros((ROWS, ROWS), F32)], axis=1) * LOG2E
            norm_t[...] = jnp.concatenate([block, block], axis=0).T
            for t in range(TILES):
                k_all[t] = k_ring[0, t]
                dq_t[t] = jnp.zeros((HEAD_SIZE, GROUP * TILE), F32)
            dv_pairs[PAIRS] = jnp.zeros((TILE, HEAD_SIZE), F32)
            dk_pairs[PAIRS] = jnp.zeros((TILE, HEAD_SIZE), F32)

        owner = lax.rem(h + i, NH)
        cols = columns(owner, WIDE)
        product = do_own[:, cols].astype(F32) * o_own[:, cols].astype(F32)
        block = jnp.zeros((ROWS, 128), F32)
        for g in range(GROUP):
            delta = jnp.sum(product[:, g * HEAD_SIZE : (g + 1) * HEAD_SIZE], axis=1, keepdims=True)
            block = jnp.where(lane == g, delta, block)
        turned = jnp.concatenate([block, block], axis=0).T
        norms = norm_t[pl.ds(pl.multiple_of(owner * GROUP, GROUP), GROUP), :]
        st_out[i, :GROUP] = jnp.where(keep, norms, 0.0)
        st_out[i, GROUP:] = jnp.where(keep, turned[:GROUP], 0.0)

        @pl.when(i > 0)
        def _():
            head_copy(ST, i).start()

        @pl.when(i == 0)
        def _():
            own_copy(ST).start()

    @pl.loop(0, HOPS)
    def _(i):
        @pl.when(i == LAG)
        def _():
            head_arrived(V)
            for t in range(TILES):
                v_all[t] = v_ring[0, t]

        for c in range(2):
            serve(0, i, c)

            @pl.when(i >= LAG)
            def _():
                serve(1, i - LAG, c)

            if c == 0:

                @pl.when(i == 0)
                def _():
                    head_start(V)

        @pl.when(i == 0)
        def _():
            head_start(Q)
            head_start(DO)

        picks(0, i)

        @pl.when(i >= LAG)
        def _():
            picks(1, i - LAG)

        prepare(i)

    gather_end(0)

    @pl.loop(HOPS, HOPS + LAG - 1)
    def _(i):
        for c in range(2):
            serve(1, i - LAG, c)
        picks(1, i - LAG)

    for part in (Q, DO, ST):
        head_arrived(part)
    gathered(0)

    @pl.loop(0, PAIRS // 2)
    def _(b):
        first_half(b)

        @pl.when(b == 3)
        def _():
            serve(1, b - 3 + HOPS - 1, 0)

        @pl.when(b == 5)
        def _():
            serve(1, b - 5 + HOPS - 1, 1)
            picks(1, b - 5 + HOPS - 1)

        @pl.when(b == 11)
        def _():
            gather_end(1)

    reduce_start(1)
    gathered(1)

    @pl.loop(0, HOPS + BACK_LAG)
    def _(i):
        first, second = i < HOPS, i >= BACK_LAG
        j = i - BACK_LAG

        @pl.when(i == BACK_LAG)
        def _():
            reduce_start(0)

        @pl.when(i == HOPS)
        def _():
            reduce_end(1)
            head_start(GV)

        @pl.when(first)
        def _():
            take(1, i)

        for c in range(2):

            @pl.when(first)
            def _():
                hops(1, i, c)
                if c == 1:
                    give_next(1, i)

            if c == 0:

                @pl.when(second)
                def _():
                    take(0, j)

            @pl.when(second)
            def _():
                hops(0, j, c)
                if c == 1:
                    give_next(0, j)

            @pl.when(i < BACK_LAG)
            def _():
                @pl.loop(0, (PER_HOP + 1 - c) // 2)
                def _(n):
                    b = i * PER_HOP + c * ((PER_HOP + 1) // 2) + n

                    @pl.when(b < PAIRS // 2)
                    def _():
                        second_half(b)

        @pl.when(second & (j < TILES))
        def _():
            rows = pl.ds(pl.multiple_of(j * TILE, TILE), TILE)
            for g in range(GROUP):
                part = dq_t[j, :, g * TILE : (g + 1) * TILE] * SCALE
                dq_out[rows, g * HEAD_SIZE : (g + 1) * HEAD_SIZE] = part.T.astype(BF16)

        @pl.when(j == TILES - 1)
        def _():
            head_start(GQ)

    reduce_end(0)
    head_start(GK)

    for w in range(2):

        @pl.loop(1, HOPS)
        def _(j, w=w):
            for dy in range(1, NY):
                across_copy(w, j, dy, 2).wait_send()
                cross_back(w, j, dy, 2).wait_send()

        for j in (0, HOPS):
            for dy in range(1, NY):
                across_copy(w, j, dy, 1).wait_send()
                cross_back(w, j, dy, 1).wait_send()

        for j in range(HOPS):
            for c in range(2):
                if j < HOPS - 1 or c == 0:
                    up_copy(w, j, c).wait_send()
                if j < HOPS - 1 or c == 1:
                    down_copy(w, j, c).wait_send()
                if j > 0 or c == 0:
                    down_back(w, j, c).wait_send()
                if j > 0 or c == 1:
                    up_back(w, j, c).wait_send()

    for part in (GV, GQ, GK):
        head_arrived(part)
    for part in range(8):
        head_sent(part)


PIECES = 4


def hand_over(gq_ref, gk_ref, gv_ref, gq_out, gk_out, gv_out):
    gq_out[...] = gq_ref[...]
    gk_out[...] = gk_ref[...]
    gv_out[...] = gv_ref[...]


def any_spec():
    return pl.BlockSpec(memory_space=pl.ANY)


def shape(dims, dtype):
    return jax.ShapeDtypeStruct(dims, dtype)


def on_device(queries, outputs, output_gradient, keys, values, log_row_norm, kv_index, counts):
    dma = pltpu.SemaphoreType.DMA
    vmem = pltpu.VMEM
    listed = jnp.arange(ENTRIES, dtype=jnp.int32)[None, :] < counts[:, None]
    lists = jnp.where(listed, kv_index, -1).reshape(NZ * NY, PAIRS)
    padded = jnp.pad(lists, ((0, 0), (0, 128 - PAIRS)), constant_values=-1)

    node = lax.axis_index("ctx")
    tile = lax.dynamic_index_in_dim(lists, node, 0, keepdims=False)
    holder = tile // TILES
    away = (node // NY - holder // NY) % NZ
    slot = (jnp.minimum(away, NZ - away) * NY + (node - holder) % NY) * 2 + (away > HOPS)
    place = jnp.where(holder == node, tile % TILES, TILES + slot)
    place = jnp.where(tile < 0, 0, place)
    number = jnp.arange(PAIRS, dtype=jnp.int32)
    limit = jnp.where(tile == node * TILES + number // ENTRIES, 0, TILE)
    limit = jnp.where(tile < 0, -TILE, limit)
    match = (place.reshape(TILES, 1, ENTRIES) == jnp.arange(PLACES, dtype=jnp.int32)[None, :, None]) & (
        tile >= 0
    ).reshape(TILES, 1, ENTRIES)
    pair = jnp.min(jnp.where(match, number.reshape(TILES, 1, ENTRIES), PAIRS), axis=2).reshape(-1)
    meta = jnp.concatenate([place, limit, pair]).reshape(1, -1)

    block = (TILE, HEAD_SIZE)
    grads = pl.pallas_call(
        kernel,
        out_shape=(
            shape((ROWS, NH * WIDE), BF16),
            shape((ROWS, NH * HEAD_SIZE), BF16),
            shape((ROWS, NH * HEAD_SIZE), BF16),
        ),
        in_specs=[any_spec()] * 5
        + [pl.BlockSpec(memory_space=pltpu.VMEM)] * 2
        + [pl.BlockSpec(memory_space=pltpu.SMEM)],
        out_specs=(any_spec(),) * 3,
        scratch_shapes=[
            vmem((NZ, TILES) + block, BF16), vmem((NZ, TILES) + block, BF16),
            vmem((PLACES,) + block, BF16), vmem((PLACES,) + block, BF16),
            vmem((2, HOPS + 1, NY - 1, 2) + block, BF16),
            vmem((NH * ROWS, WIDE), BF16), vmem((NH * ROWS, WIDE), BF16),
            vmem((ROWS, NH * WIDE), BF16), vmem((ROWS, NH * WIDE), BF16),
            vmem(block, F32), vmem((NH, 2 * GROUP, 128), F32), vmem((NH, 2 * GROUP, 128), F32),
            vmem((NY, NZ, 128), jnp.int32),
            vmem((PAIRS, TILE, GROUP * TILE), F32),
            vmem((PAIRS + 1,) + block, F32), vmem((PAIRS + 1,) + block, F32),
            vmem((TILES, HEAD_SIZE, GROUP * TILE), F32), vmem((NH * ROWS, WIDE), BF16),
            vmem((2, HOPS + 1, NY, 2) + block, BF16),
            vmem((HOPS + 1, NY - 1, 2) + block, BF16), vmem((HOPS + 1, NY - 1, 2) + block, BF16),
            vmem((2, HOPS, TILES) + block, BF16), vmem((2, HOPS, TILES) + block, BF16),
            vmem((HOPS, TILES) + block, BF16), vmem((HOPS, TILES) + block, BF16),
            vmem((HOPS, TILES) + block, BF16), vmem((HOPS, TILES) + block, BF16),
            vmem((TILES,) + block, BF16), vmem((TILES,) + block, BF16),
            dma((8, NH - 1)), dma((8, NH - 1)), dma((8,)), dma((2,)),
            dma((2, HOPS, 2)), dma((2, HOPS, 2)), dma((2, HOPS, 2)), dma((2, HOPS, 2)),
            dma((2, HOPS + 1, NY - 1)), dma((2, HOPS + 1, NY - 1)),
            dma((2, HOPS, 2)), dma((2, HOPS, 2)), dma((2, HOPS, 2)), dma((2, HOPS, 2)),
            dma((2, HOPS + 1, NY - 1)), dma((2, HOPS + 1, NY - 1)),
        ],
        compiler_params=pltpu.CompilerParams(collective_id=0, has_side_effects=True, vmem_limit_bytes=63 << 20),
        cost_estimate=pl.CostEstimate(flops=6_710_886_400, bytes_accessed=12 << 20, transcendentals=5_242_880),
        name="attention_backward",
    )(queries, outputs, output_gradient, keys, values, log_row_norm, padded, meta)
    return pl.pallas_call(
        hand_over,
        out_shape=tuple(shape(grad.shape, grad.dtype) for grad in grads),
        grid=(PIECES,),
        in_specs=[pl.BlockSpec((ROWS // PIECES, grad.shape[1]), lambda i: (i, 0)) for grad in grads],
        out_specs=tuple(pl.BlockSpec((ROWS // PIECES, grad.shape[1]), lambda i: (i, 0)) for grad in grads),
        name="hand_over",
    )(*grads)


def solution(mesh):
    rows = P(("ctx", "head"), None)
    return jax.shard_map(
        on_device,
        mesh=mesh,
        in_specs=(rows,) * 6 + (P(), P()),
        out_specs=(rows,) * 3,
        check_vma=False,
    )
```

```python
import math

import jax
import jax.numpy as jnp
from jax import lax
from jax.experimental import pallas as pl
from jax.experimental.pallas import tpu as pltpu
from jax.sharding import PartitionSpec as P

QUERY_HEADS = 64
KEY_VALUE_HEADS = 8
HEAD_SIZE = 128
TILE = 128
GROUP = QUERY_HEADS // KEY_VALUE_HEADS
TILES = 4
ENTRIES = 10
PAIRS = TILES * ENTRIES
NZ = 16
NY = 4
NH = 8
HOPS = NZ // 2
PLACES = TILES + (HOPS + 1) * NY * 2
LAG = 2
BACK_LAG = 2
PER_HOP = -(-PAIRS // 2 // BACK_LAG)
CHUNK = TILES // 2
ROWS = 64
WIDE = GROUP * HEAD_SIZE
SCALE = HEAD_SIZE ** (-0.5)
LOG2E = math.log2(math.e)
MESH = pl.DeviceIdType.MESH
F32 = jnp.float32
BF16 = jnp.bfloat16
NT = (((1,), (1,)), ((), ()))
TN = (((0,), (0,)), ((), ()))

K, V, Q, DO, ST, GQ, GV, GK = range(8)


def kernel(
    q_ref, o_ref, do_ref, k_ref, v_ref, norm_ref, lists_ref, meta_ref,
    gq_ref, gk_ref, gv_ref,
    k_ring, v_ring, k_all, v_all, picked, q_all, do_all, o_own, do_own, norm_t, st_out, st_all, sel,
    weights, dv_pairs, dk_pairs, dq_t, dq_out, terms, dv_across, dk_across, down_out, up_out,
    dv_down, dv_up, dk_down, dk_up, dv_done, dk_done,
    x_send, x_recv, local, own_sem,
    u_send, u_recv, d_send, d_recv, y_send, y_recv,
    bu_send, bu_recv, bd_send, bd_recv, by_send, by_recv,
):
    ctx = lax.axis_index("ctx")
    h, z, y = lax.axis_index("head"), ctx // NY, lax.rem(ctx, NY)
    above = lax.rem(z + 1, NZ) * NY + y
    below = lax.rem(z + NZ - 1, NZ) * NY + y

    barrier = pltpu.get_barrier_semaphore()

    def greet(**where):
        pl.semaphore_signal(barrier, inc=1, device_id=where, device_id_type=MESH)

    for d in range(1, NH):
        greet(head=lax.rem(h + d, NH))
    for d in range(1, NY):
        greet(ctx=z * NY + lax.rem(y + d, NY))
    greet(ctx=above)
    greet(ctx=below)

    own_load = [
        pltpu.make_async_copy(o_ref, o_own, own_sem.at[0]),
        pltpu.make_async_copy(do_ref, do_own, own_sem.at[1]),
    ]
    for copy in own_load:
        copy.start()
    pl.semaphore_wait(barrier, NH + NY)

    def columns(owner, width):
        return pl.ds(pl.multiple_of(owner * width, width), width)

    def half(owner):
        return pl.ds(pl.multiple_of(lax.rem(owner, 2) * ROWS, ROWS), ROWS)

    def rows_of(owner):
        return pl.ds(pl.multiple_of(owner * ROWS, ROWS), ROWS)

    def head_ends(part, owner, d):
        if part == K:
            return k_ref.at[:, columns(owner, HEAD_SIZE)], k_ring.at[0, h // 2, half(h), :]
        if part == V:
            return v_ref.at[:, columns(owner, HEAD_SIZE)], v_ring.at[0, h // 2, half(h), :]
        if part == Q:
            return q_ref.at[:, columns(owner, WIDE)], q_all.at[rows_of(h), :]
        if part == DO:
            return do_ref.at[:, columns(owner, WIDE)], do_all.at[rows_of(h), :]
        if part == ST:
            return st_out.at[d], st_all.at[h]
        if part == GQ:
            return dq_out.at[rows_of(owner), :], gq_ref.at[:, columns(h, WIDE)]
        if part == GV:
            return dv_done.at[owner // 2, half(owner), :], gv_ref.at[:, columns(h, HEAD_SIZE)]
        return dk_done.at[owner // 2, half(owner), :], gk_ref.at[:, columns(h, HEAD_SIZE)]

    def head_copy(part, d):
        owner = lax.rem(h + d, NH)
        src, dst = head_ends(part, owner, d)
        return pltpu.make_async_remote_copy(
            src_ref=src, dst_ref=dst, send_sem=x_send.at[part, d - 1], recv_sem=x_recv.at[part, d - 1],
            device_id={"head": owner}, device_id_type=MESH,
        )

    def own_copy(part):
        src, dst = head_ends(part, h, 0)
        return pltpu.make_async_copy(src, dst, local.at[part])

    def head_start(part):
        for d in range(1, NH):
            head_copy(part, d).start()
        own_copy(part).start()

    def head_arrived(part):
        own_copy(part).wait()
        for d in range(1, NH):
            head_copy(part, d).wait_recv()

    def head_sent(part):
        for d in range(1, NH):
            head_copy(part, d).wait_send()

    ring_of, all_of = (k_ring, v_ring), (k_all, v_all)

    def tiles(c):
        return pl.ds(c * CHUNK, CHUNK)

    def up_copy(w, j, c):
        ring = ring_of[w]
        return pltpu.make_async_remote_copy(
            src_ref=ring.at[j, tiles(c)], dst_ref=ring.at[j + 1, tiles(c)],
            send_sem=u_send.at[w, j, c], recv_sem=u_recv.at[w, j, c],
            device_id={"ctx": above}, device_id_type=MESH,
        )

    def down_copy(w, j, c):
        ring = ring_of[w]
        return pltpu.make_async_remote_copy(
            src_ref=ring.at[lax.rem(NZ - j, NZ), tiles(c)], dst_ref=ring.at[NZ - 1 - j, tiles(c)],
            send_sem=d_send.at[w, j, c], recv_sem=d_recv.at[w, j, c],
            device_id={"ctx": below}, device_id_type=MESH,
        )

    def across_copy(w, j, dy, sides):
        return pltpu.make_async_remote_copy(
            src_ref=picked.at[w, j, dy - 1, pl.ds(0, sides)],
            dst_ref=all_of[w].at[pl.ds(TILES + (j * NY + dy) * 2, sides)],
            send_sem=y_send.at[w, j, dy - 1], recv_sem=y_recv.at[w, j, dy - 1],
            device_id={"ctx": z * NY + lax.rem(y + dy, NY)}, device_id_type=MESH,
        )

    def pick(w, s, j, side):
        ring = ring_of[w]
        for dy in range(NY):
            want = sel[dy, pl.ds(s, 1), :]
            for c in range(TILES):
                term = ring[s, c] * (want == c).astype(F32).astype(BF16)
                total = term if c == 0 else total + term
            if dy == 0:
                all_of[w][TILES + j * NY * 2 + side] = total
            else:
                picked[w, j, dy - 1, side] = total

    def picks(w, j):
        pick(w, j, j, 0)

        @pl.when(j > 0)
        def _():
            pick(w, NZ - j, j, 1)
            for dy in range(1, NY):
                across_copy(w, j, dy, 2).start()

        @pl.when(j == 0)
        def _():
            for dy in range(1, NY):
                across_copy(w, j, dy, 1).start()

    def serve(w, j, c):
        @pl.when(j > 0)
        def _():
            up_copy(w, j - 1, c).wait_recv()

        @pl.when((j < HOPS - 1) | (c == 0))
        def _():
            up_copy(w, j, c).start()

        @pl.when(j > 0)
        def _():
            down_copy(w, j - 1, c).wait_recv()

        @pl.when((j < HOPS - 1) | (c == 1))
        def _():
            down_copy(w, j, c).start()

    def gather_end(w):
        up_copy(w, HOPS - 1, 0).wait_recv()
        down_copy(w, HOPS - 1, 1).wait_recv()
        pick(w, HOPS, HOPS, 0)
        for dy in range(1, NY):
            across_copy(w, HOPS, dy, 1).start()

    def gathered(w):
        @pl.loop(1, HOPS)
        def _(j):
            for dy in range(1, NY):
                across_copy(w, j, dy, 2).wait_recv()

        for j in (0, HOPS):
            for dy in range(1, NY):
                across_copy(w, j, dy, 1).wait_recv()

    order = lax.broadcasted_iota(jnp.int32, (TILE, GROUP * TILE), 0) - lax.rem(
        lax.broadcasted_iota(jnp.int32, (TILE, GROUP * TILE), 1), TILE
    )

    def all_heads(ref, t):
        rows = pl.ds(pl.multiple_of(t * TILE, TILE), TILE)
        return jnp.concatenate([ref[rows, g * HEAD_SIZE : (g + 1) * HEAD_SIZE] for g in range(GROUP)], axis=0)

    def stat_rows(t, first):
        both = st_all[2 * t] + st_all[2 * t + 1]
        return jnp.concatenate([both[first + g : first + g + 1] for g in range(GROUP)], axis=1)

    def two_tiles(ref, e):
        return jnp.concatenate([ref[meta_ref[0, e]], ref[meta_ref[0, e + 1]]], axis=0)

    def first_half(b):
        e = 2 * b
        t = e // ENTRIES
        scores = lax.dot_general(two_tiles(k_all, e), all_heads(q_all, t), NT, preferred_element_type=F32)
        full = jnp.exp2(scores * (SCALE * LOG2E) - stat_rows(t, 0))
        parts = []
        for i in range(2):
            part = jnp.where(order <= meta_ref[0, PAIRS + e + i], full[i * TILE : (i + 1) * TILE], 0.0)
            weights[e + i] = part
            parts.append(part.astype(BF16))
        dv = jnp.dot(jnp.concatenate(parts, axis=0), all_heads(do_all, t), preferred_element_type=F32)
        for i in range(2):
            dv_pairs[e + i] = dv[i * TILE : (i + 1) * TILE]

    def second_half(b):
        e = 2 * b
        t = e // ENTRIES
        dp = lax.dot_general(two_tiles(v_all, e), all_heads(do_all, t), NT, preferred_element_type=F32)
        delta = stat_rows(t, GROUP)
        parts = [(weights[e + i] * (dp[i * TILE : (i + 1) * TILE] - delta)).astype(BF16) for i in range(2)]
        score_grad = jnp.concatenate(parts, axis=0)
        dk = jnp.dot(score_grad, all_heads(q_all, t), preferred_element_type=F32) * SCALE
        for i in range(2):
            dk_pairs[e + i] = dk[i * TILE : (i + 1) * TILE]
            weights[e + i] = parts[i].astype(F32)

    def query_part(b):
        e = 2 * b
        score_grad = jnp.concatenate([weights[e], weights[e + 1]], axis=0).astype(BF16)
        dq_t[e // ENTRIES] += lax.dot_general(two_tiles(k_all, e), score_grad, TN, preferred_element_type=F32)

    pairs_of, cross_of, done_of = (dk_pairs, dv_pairs), (dk_across, dv_across), (dk_done, dv_done)
    down_of, up_of = (dk_down, dv_down), (dk_up, dv_up)

    def cross_back(w, j, dy, sides):
        return pltpu.make_async_remote_copy(
            src_ref=terms.at[w, j, dy, pl.ds(0, sides)], dst_ref=cross_of[w].at[j, dy - 1, pl.ds(0, sides)],
            send_sem=by_send.at[w, j, dy - 1], recv_sem=by_recv.at[w, j, dy - 1],
            device_id={"ctx": z * NY + lax.rem(y + NY - dy, NY)}, device_id_type=MESH,
        )

    def down_back(w, j, c):
        return pltpu.make_async_remote_copy(
            src_ref=down_out.at[w, j, tiles(c)], dst_ref=down_of[w].at[j, tiles(c)],
            send_sem=bd_send.at[w, j, c], recv_sem=bd_recv.at[w, j, c],
            device_id={"ctx": below}, device_id_type=MESH,
        )

    def up_back(w, j, c):
        return pltpu.make_async_remote_copy(
            src_ref=up_out.at[w, j, tiles(c)], dst_ref=up_of[w].at[j, tiles(c)],
            send_sem=bu_send.at[w, j, c], recv_sem=bu_recv.at[w, j, c],
            device_id={"ctx": above}, device_id_type=MESH,
        )

    def place_sum(w, place):
        for t in range(TILES):
            term = pairs_of[w][meta_ref[0, 2 * PAIRS + t * PLACES + place]]
            total = term if t == 0 else total + term
        return total

    def give(w, j, sides):
        for dy in range(NY):
            for side in range(sides):
                terms[w, j, dy, side] = place_sum(w, TILES + (j * NY + dy) * 2 + side).astype(BF16)
            if dy > 0:
                cross_back(w, j, dy, sides).start()

    def taken(w, j, sides):
        for dy in range(1, NY):
            cross_back(w, j, dy, sides).wait_recv()

    def asked(w, s, j, side, c, first):
        total = None
        for dy in range(first, NY):
            weight = (sel[dy, pl.ds(s, 1), :] == c).astype(F32)
            block = terms[w, j, 0, side] if dy == 0 else cross_of[w][j, dy - 1, side]
            term = block.astype(F32) * weight
            total = term if total is None else total + term
        return total

    def reduce_start(w):
        give(w, HOPS, 1)
        for j in (HOPS - 1, HOPS - 2):
            give(w, j, 2)
        for c in range(CHUNK):
            down_of[w][0, CHUNK + c] = jnp.zeros((TILE, HEAD_SIZE), BF16)
            up_of[w][0, c] = jnp.zeros((TILE, HEAD_SIZE), BF16)

    def hop(w, j, c, out, into, side, copy, first):
        slot = HOPS + j if side == 1 else HOPS - j

        if c == first:

            @pl.when(j == 0)
            def _():
                for i in range(c * CHUNK, (c + 1) * CHUNK):
                    out[w, 0, i] = asked(w, HOPS, HOPS, 0, i, 0).astype(BF16)
                copy(w, j, c).start()

            @pl.when(j > 0)
            def _():
                copy(w, j - 1, c).wait_recv()

        else:

            @pl.when(j > 1)
            def _():
                copy(w, j - 1, c).wait_recv()

        @pl.when(j > 0)
        def _():
            for i in range(c * CHUNK, (c + 1) * CHUNK):
                part = asked(w, slot, HOPS - j, side, i, 0)
                out[w, j, i] = (part + into[j - 1, i].astype(F32)).astype(BF16)
            copy(w, j, c).start()

    def take(w, j):
        @pl.when(j == 0)
        def _():
            taken(w, HOPS - j, 1)

        @pl.when(j > 0)
        def _():
            taken(w, HOPS - j, 2)

    def hops(w, j, c):
        hop(w, j, c, down_out, down_of[w], 0, down_back, 0)
        hop(w, j, c, up_out, up_of[w], 1, up_back, 1)

    def give_next(w, j):
        @pl.when(j < HOPS - 3)
        def _():
            give(w, HOPS - 3 - j, 2)

        @pl.when(j == HOPS - 3)
        def _():
            give(w, HOPS - 3 - j, 1)

    def reduce_end(w):
        taken(w, 0, 1)
        for i in range(TILES):
            c = i // CHUNK
            part = place_sum(w, i) + asked(w, 0, 0, 0, i, 1)
            if i % CHUNK == 0:
                down_back(w, HOPS - 1, c).wait_recv()
                up_back(w, HOPS - 1, c).wait_recv()
            part += down_of[w][HOPS - 1, i].astype(F32)
            part += up_of[w][HOPS - 1, i].astype(F32)
            done_of[w][i] = part.astype(BF16)

    head_start(K)
    slot = lax.broadcasted_iota(jnp.int32, (NZ, 128), 0)
    plane = lax.rem(z - slot + NZ, NZ)
    for dy in range(NY):
        node = z * NY + lax.rem(y + dy, NY)
        entries = lists_ref[pl.ds(node, 1), :]
        match = (entries >> 2) == plane * NY + y
        found = jnp.max(jnp.where(match, entries & 3, -1), axis=1, keepdims=True)
        sel[dy] = jnp.broadcast_to(found, (NZ, 128))
    head_arrived(K)

    lane = lax.broadcasted_iota(jnp.int32, (ROWS, 128), 1)
    keep = (lax.broadcasted_iota(jnp.int32, (GROUP, 128), 1) >= ROWS) == (lax.rem(h, 2) == 1)

    def prepare(i):
        @pl.when(i == 0)
        def _():
            for copy in own_load:
                copy.wait()
            block = jnp.concatenate([norm_ref[...], jnp.zeros((ROWS, ROWS), F32)], axis=1) * LOG2E
            norm_t[...] = jnp.concatenate([block, block], axis=0).T
            for t in range(TILES):
                k_all[t] = k_ring[0, t]
                dq_t[t] = jnp.zeros((HEAD_SIZE, GROUP * TILE), F32)
            dv_pairs[PAIRS] = jnp.zeros((TILE, HEAD_SIZE), F32)
            dk_pairs[PAIRS] = jnp.zeros((TILE, HEAD_SIZE), F32)

        owner = lax.rem(h + i, NH)
        cols = columns(owner, WIDE)
        product = do_own[:, cols].astype(F32) * o_own[:, cols].astype(F32)
        block = jnp.zeros((ROWS, 128), F32)
        for g in range(GROUP):
            delta = jnp.sum(product[:, g * HEAD_SIZE : (g + 1) * HEAD_SIZE], axis=1, keepdims=True)
            block = jnp.where(lane == g, delta, block)
        turned = jnp.concatenate([block, block], axis=0).T
        norms = norm_t[pl.ds(pl.multiple_of(owner * GROUP, GROUP), GROUP), :]
        st_out[i, :GROUP] = jnp.where(keep, norms, 0.0)
        st_out[i, GROUP:] = jnp.where(keep, turned[:GROUP], 0.0)

        @pl.when(i > 0)
        def _():
            head_copy(ST, i).start()

        @pl.when(i == 0)
        def _():
            own_copy(ST).start()

    @pl.loop(0, HOPS)
    def _(i):
        @pl.when(i == LAG)
        def _():
            head_arrived(V)
            for t in range(TILES):
                v_all[t] = v_ring[0, t]

        for c in range(2):
            serve(0, i, c)

            @pl.when(i >= LAG)
            def _():
                serve(1, i - LAG, c)

            if c == 0:

                @pl.when(i == 0)
                def _():
                    head_start(V)

                @pl.when(i > LAG)
                def _():
                    picks(1, i - 1 - LAG)

        @pl.when(i == 0)
        def _():
            head_start(Q)
            head_start(DO)

        picks(0, i)
        prepare(i)

    gather_end(0)

    @pl.loop(HOPS, HOPS + LAG - 1)
    def _(i):
        for c in range(2):
            serve(1, i - LAG, c)
            if c == 0:
                picks(1, i - 1 - LAG)

    for part in (Q, DO, ST):
        head_arrived(part)
    gathered(0)

    @pl.loop(0, PAIRS // 2)
    def _(b):
        first_half(b)

        @pl.when(b == 3)
        def _():
            serve(1, b - 3 + HOPS - 1, 0)
            picks(1, b - 3 + HOPS - 2)

        @pl.when(b == 5)
        def _():
            serve(1, b - 5 + HOPS - 1, 1)
            picks(1, b - 5 + HOPS - 1)

        @pl.when(b == 11)
        def _():
            gather_end(1)

    reduce_start(1)
    gathered(1)

    @pl.loop(0, HOPS + BACK_LAG)
    def _(i):
        first, second = i < HOPS, i >= BACK_LAG
        j = i - BACK_LAG

        @pl.when(i == BACK_LAG)
        def _():
            reduce_start(0)

        @pl.when(i == HOPS)
        def _():
            reduce_end(1)
            head_start(GV)

        @pl.when(first)
        def _():
            take(1, i)

        for c in range(2):

            @pl.when(first)
            def _():
                hops(1, i, c)
                if c == 0:
                    give_next(1, i)

            if c == 0:

                @pl.when(second)
                def _():
                    take(0, j)

            @pl.when(second)
            def _():
                hops(0, j, c)
                if c == 1:
                    give_next(0, j)

            @pl.when(i < BACK_LAG)
            def _():
                @pl.loop(0, (PER_HOP + 1 - c) // 2)
                def _(n):
                    b = i * PER_HOP + c * ((PER_HOP + 1) // 2) + n

                    @pl.when(b < PAIRS // 2)
                    def _():
                        second_half(b)

        @pl.when(second & (j < TILES))
        def _():
            @pl.loop(0, ENTRIES // 2)
            def _(n):
                query_part(j * (ENTRIES // 2) + n)

            rows = pl.ds(pl.multiple_of(j * TILE, TILE), TILE)
            for g in range(GROUP):
                part = dq_t[j, :, g * TILE : (g + 1) * TILE] * SCALE
                dq_out[rows, g * HEAD_SIZE : (g + 1) * HEAD_SIZE] = part.T.astype(BF16)

        @pl.when(j == TILES - 1)
        def _():
            head_start(GQ)

    reduce_end(0)
    head_start(GK)

    for w in range(2):

        @pl.loop(1, HOPS)
        def _(j, w=w):
            for dy in range(1, NY):
                across_copy(w, j, dy, 2).wait_send()
                cross_back(w, j, dy, 2).wait_send()

        for j in (0, HOPS):
            for dy in range(1, NY):
                across_copy(w, j, dy, 1).wait_send()
                cross_back(w, j, dy, 1).wait_send()

        for j in range(HOPS):
            for c in range(2):
                if j < HOPS - 1 or c == 0:
                    up_copy(w, j, c).wait_send()
                if j < HOPS - 1 or c == 1:
                    down_copy(w, j, c).wait_send()
                if j > 0 or c == 0:
                    down_back(w, j, c).wait_send()
                if j > 0 or c == 1:
                    up_back(w, j, c).wait_send()

    for part in (GV, GQ, GK):
        head_arrived(part)
    for part in range(8):
        head_sent(part)


PIECES = 4


def hand_over(gq_ref, gk_ref, gv_ref, gq_out, gk_out, gv_out):
    gq_out[...] = gq_ref[...]
    gk_out[...] = gk_ref[...]
    gv_out[...] = gv_ref[...]


def any_spec():
    return pl.BlockSpec(memory_space=pl.ANY)


def shape(dims, dtype):
    return jax.ShapeDtypeStruct(dims, dtype)


def on_device(queries, outputs, output_gradient, keys, values, log_row_norm, kv_index, counts):
    dma = pltpu.SemaphoreType.DMA
    vmem = pltpu.VMEM
    listed = jnp.arange(ENTRIES, dtype=jnp.int32)[None, :] < counts[:, None]
    lists = jnp.where(listed, kv_index, -1).reshape(NZ * NY, PAIRS)
    padded = jnp.pad(lists, ((0, 0), (0, 128 - PAIRS)), constant_values=-1)

    node = lax.axis_index("ctx")
    tile = lax.dynamic_index_in_dim(lists, node, 0, keepdims=False)
    holder = tile // TILES
    away = (node // NY - holder // NY) % NZ
    slot = (jnp.minimum(away, NZ - away) * NY + (node - holder) % NY) * 2 + (away > HOPS)
    place = jnp.where(holder == node, tile % TILES, TILES + slot)
    place = jnp.where(tile < 0, 0, place)
    number = jnp.arange(PAIRS, dtype=jnp.int32)
    limit = jnp.where(tile == node * TILES + number // ENTRIES, 0, TILE)
    limit = jnp.where(tile < 0, -TILE, limit)
    match = (place.reshape(TILES, 1, ENTRIES) == jnp.arange(PLACES, dtype=jnp.int32)[None, :, None]) & (
        tile >= 0
    ).reshape(TILES, 1, ENTRIES)
    pair = jnp.min(jnp.where(match, number.reshape(TILES, 1, ENTRIES), PAIRS), axis=2).reshape(-1)
    meta = jnp.concatenate([place, limit, pair]).reshape(1, -1)

    block = (TILE, HEAD_SIZE)
    grads = pl.pallas_call(
        kernel,
        out_shape=(
            shape((ROWS, NH * WIDE), BF16),
            shape((ROWS, NH * HEAD_SIZE), BF16),
            shape((ROWS, NH * HEAD_SIZE), BF16),
        ),
        in_specs=[any_spec()] * 5
        + [pl.BlockSpec(memory_space=pltpu.VMEM)] * 2
        + [pl.BlockSpec(memory_space=pltpu.SMEM)],
        out_specs=(any_spec(),) * 3,
        scratch_shapes=[
            vmem((NZ, TILES) + block, BF16), vmem((NZ, TILES) + block, BF16),
            vmem((PLACES,) + block, BF16), vmem((PLACES,) + block, BF16),
            vmem((2, HOPS + 1, NY - 1, 2) + block, BF16),
            vmem((NH * ROWS, WIDE), BF16), vmem((NH * ROWS, WIDE), BF16),
            vmem((ROWS, NH * WIDE), BF16), vmem((ROWS, NH * WIDE), BF16),
            vmem(block, F32), vmem((NH, 2 * GROUP, 128), F32), vmem((NH, 2 * GROUP, 128), F32),
            vmem((NY, NZ, 128), jnp.int32),
            vmem((PAIRS, TILE, GROUP * TILE), F32),
            vmem((PAIRS + 1,) + block, F32), vmem((PAIRS + 1,) + block, F32),
            vmem((TILES, HEAD_SIZE, GROUP * TILE), F32), vmem((NH * ROWS, WIDE), BF16),
            vmem((2, HOPS + 1, NY, 2) + block, BF16),
            vmem((HOPS + 1, NY - 1, 2) + block, BF16), vmem((HOPS + 1, NY - 1, 2) + block, BF16),
            vmem((2, HOPS, TILES) + block, BF16), vmem((2, HOPS, TILES) + block, BF16),
            vmem((HOPS, TILES) + block, BF16), vmem((HOPS, TILES) + block, BF16),
            vmem((HOPS, TILES) + block, BF16), vmem((HOPS, TILES) + block, BF16),
            vmem((TILES,) + block, BF16), vmem((TILES,) + block, BF16),
            dma((8, NH - 1)), dma((8, NH - 1)), dma((8,)), dma((2,)),
            dma((2, HOPS, 2)), dma((2, HOPS, 2)), dma((2, HOPS, 2)), dma((2, HOPS, 2)),
            dma((2, HOPS + 1, NY - 1)), dma((2, HOPS + 1, NY - 1)),
            dma((2, HOPS, 2)), dma((2, HOPS, 2)), dma((2, HOPS, 2)), dma((2, HOPS, 2)),
            dma((2, HOPS + 1, NY - 1)), dma((2, HOPS + 1, NY - 1)),
        ],
        compiler_params=pltpu.CompilerParams(collective_id=0, has_side_effects=True, vmem_limit_bytes=63 << 20),
        cost_estimate=pl.CostEstimate(flops=6_710_886_400, bytes_accessed=12 << 20, transcendentals=5_242_880),
        name="attention_backward",
    )(queries, outputs, output_gradient, keys, values, log_row_norm, padded, meta)
    return pl.pallas_call(
        hand_over,
        out_shape=tuple(shape(grad.shape, grad.dtype) for grad in grads),
        grid=(PIECES,),
        in_specs=[pl.BlockSpec((ROWS // PIECES, grad.shape[1]), lambda i: (i, 0)) for grad in grads],
        out_specs=tuple(pl.BlockSpec((ROWS // PIECES, grad.shape[1]), lambda i: (i, 0)) for grad in grads),
        name="hand_over",
    )(*grads)


def solution(mesh):
    rows = P(("ctx", "head"), None)
    return jax.shard_map(
        on_device,
        mesh=mesh,
        in_specs=(rows,) * 6 + (P(), P()),
        out_specs=(rows,) * 3,
        check_vma=False,
    )
```
